32 devices in a mesh: wide: 8 (over z, x), narrow: 4 (over y, core).
Axes of the slice: x: 2, y: 2, z: 4, core: 2. Of those that a mesh axis runs over, the one named last changes fastest.
Arguments:
- first_input: bfloat16 [512, 256, 512], P(('wide', 'narrow')), may hold values from -6 to 6
- second_input: bfloat16 [512, 256, 512], P(('wide', 'narrow')), may hold values from -6 to 6
- cotangent: bfloat16 [512, 256, 512], P(('wide', 'narrow')), may hold values from -6 to 6
- lengths: int32 [512], P(('wide', 'narrow')), may hold values from 232 to 256, as said below
- conv_weight: bfloat16 [7, 512], P(None, ('wide', 'narrow')), may hold values from -2 to 2
- conv_bias: bfloat16 [512], P(('wide', 'narrow')), may hold values from -3 to 3
- norm_gain: bfloat16 [512], P(('wide', 'narrow')), may hold values from 0.5 to 2
- norm_bias: bfloat16 [512], P(('wide', 'narrow')), may hold values from -3 to 3
- up_weight: bfloat16 [512, 1536], P(('wide', 'narrow')), may hold values from -0.25 to 0.25
- up_bias: bfloat16 [1536], P(('wide', 'narrow')), may hold values from -3 to 3
- down_weight: bfloat16 [1536, 512], P(('wide', 'narrow')), may hold values from -0.15625 to 0.15625
- down_bias: bfloat16 [512], P(('wide', 'narrow')), may hold values from -2 to 2
- layer_scale: bfloat16 [512], P(('wide', 'narrow')), may hold values from 0.29882812 to 1.5
Outputs:
- first_output: bfloat16 [512, 256, 512], P(('wide', 'narrow'))
- second_output: bfloat16 [512, 256, 512], P(('wide', 'narrow'))
- input_grad: bfloat16 [512, 256, 512], P(('wide', 'narrow'))
- grad_conv_weight: float32 [7, 512], P(None, ('wide', 'narrow'))
- grad_conv_bias: float32 [512], P(('wide', 'narrow'))
- grad_norm_gain: float32 [512], P(('wide', 'narrow'))
- grad_norm_bias: float32 [512], P(('wide', 'narrow'))
- grad_up_weight: float32 [512, 1536], P(('wide', 'narrow'))
- grad_up_bias: float32 [1536], P(('wide', 'narrow'))
- grad_down_weight: float32 [1536, 512], P(('wide', 'narrow'))
- grad_down_bias: float32 [512], P(('wide', 'narrow'))
- grad_layer_scale: float32 [512], P(('wide', 'narrow'))
The draws below stay inside these ranges and needn't reach their ends.
Inputs may be any that keep to these rules, and one draw needn't show every extreme that they name: Each clip has 256 or 232 frames; both lengths occur.
All inputs are finite; a program needn't handle non-finite values.
Results may differ from the reference program's by a relative error of at most 0.007.
Values may be sent and summed in bfloat16 or wider, within the bound.
No kernel may reach another device: no remote copies, remote signals or barrier semaphores. Data moves between devices by JAX's collectives and lax.ppermute only.
A program may use at most 256 MiB of HBM per device.

```python
import math
import jax
import jax.numpy as jnp
from jax import lax

D = 512
H = 1536
KERNEL = 7
FRAMES = 256
CLIPS = 512


def draw_lengths(key, part):
    key = jax.random.fold_in(key, 11)
    longer = jax.random.randint(key, (CLIPS,), 0, 2)
    longer = longer.at[0].set(1).at[1].set(0)
    return (FRAMES - (1 - longer) * (3 * FRAMES // 32)).astype(jnp.int32)


def level_of(key, shape, cuts, low, top_value):
    level = 1.0
    for dim, blocks in cuts:
        heights = jax.random.uniform(jax.random.fold_in(jax.random.fold_in(key, 6), dim), (blocks,), jnp.float32, low / len(cuts), top_value / len(cuts))
        level = level * jnp.repeat(jnp.exp(heights), shape[dim] // blocks).reshape((-1,) + (1,) * (len(shape) - 1 - dim))
    return level


def normal_values(own_key, extent, width, limit, shards=(), dtype=jnp.bfloat16):
    values = width * jax.random.normal(own_key, extent, jnp.float32)
    if shards:
        values = values * level_of(own_key, extent, shards, -0.22, 0.18)
    return jnp.clip(values, -limit, limit).astype(dtype)


def setup_inputs(seed: int = 0) -> dict:
    key_of = jax.random.split(jax.random.key(seed), 14)
    return {
        "first_input": normal_values(key_of[0], (CLIPS, FRAMES, D), 1.0, 6.0, ((0, 32),)),
        "second_input": normal_values(key_of[1], (CLIPS, FRAMES, D), 1.0, 6.0, ((0, 32),)),
        "cotangent": normal_values(key_of[2], (CLIPS, FRAMES, D), 1.0, 6.0, ((0, 32),)),
        "lengths": draw_lengths(jax.random.fold_in(key_of[13], 71), 0),
        "conv_weight": normal_values(key_of[4], (KERNEL, D), KERNEL ** -0.5, 2.0, ((1, 32),)),
        "conv_bias": normal_values(key_of[5], (D,), 0.5, 3.0, ((0, 32),)),
        "norm_gain": jnp.clip(jnp.exp(math.log(2.0) - 1.3862944 * jax.random.uniform(key_of[6], (D,), jnp.float32) ** level_of(key_of[6], (D,), ((0, 32),), -0.2, 0.2)), 0.5, 2.0).astype(jnp.bfloat16),
        "norm_bias": normal_values(key_of[7], (D,), 0.5, 3.0, ((0, 32),)),
        "up_weight": normal_values(key_of[8], (D, H), D ** -0.5, 0.25, ((0, 32),)),
        "up_bias": normal_values(key_of[9], (H,), 0.5, 3.0, ((0, 32),)),
        "down_weight": normal_values(key_of[10], (H, D), H ** -0.5, 0.15625, ((0, 32),)),
        "down_bias": normal_values(key_of[11], (D,), 0.3, 2.0, ((0, 32),)),
        "layer_scale": jnp.clip(jnp.exp(math.log(1.5) - 1.6133518 * jax.random.uniform(key_of[12], (D,), jnp.float32) ** level_of(key_of[12], (D,), ((0, 32),), -0.2, 0.2)), 0.29882812, 1.5).astype(jnp.bfloat16),
    }


@jax.custom_vjp
def low(v):
    return lax.optimization_barrier(v.astype(jnp.bfloat16)).astype(jnp.float32)

@jax.custom_vjp
def low_back(v):
    return v

def low_keep(v):
    return (low(v), None)

def low_pass(kept, grad):
    return (grad,)

def back_keep(v):
    return (v, None)

def back_low(kept, grad):
    return (low(grad),)
low.defvjp(low_keep, low_pass)
low_back.defvjp(back_keep, back_low)
highest = lax.Precision.HIGHEST

def depthwise(masked, kernel_taps, conv_bias):
    margin = kernel_taps.shape[0] // 2
    frames = masked.shape[1]
    padded = jnp.pad(masked, ((0, 0), (margin, margin), (0, 0)))
    result = conv_bias + jnp.zeros_like(masked)
    for offset in range(kernel_taps.shape[0]):
        result = result + kernel_taps[offset] * padded[:, offset:offset + frames]
    return result

def normalize(conv_out, norm_gain, norm_bias):
    average = lax.optimization_barrier(jnp.mean(conv_out, axis=-1, keepdims=True))
    centred = conv_out - average
    variance = lax.optimization_barrier(jnp.mean(centred * centred, axis=-1, keepdims=True))
    return centred * lax.rsqrt(variance + 1e-06) * norm_gain + norm_bias

def forward(inputs, validity, params):
    conv_weight, conv_bias, norm_gain, norm_bias, up_weight, up_bias, down_weight, down_bias, layer_scale = params
    masked = inputs * validity
    normed = low(normalize(depthwise(masked, conv_weight, conv_bias), norm_gain, norm_bias))
    hidden = low_back(jnp.einsum('cfd,dh->cfh', normed, up_weight, precision=highest) + up_bias)
    active = low(jax.nn.gelu(hidden, approximate=False))
    branch = low_back(jnp.einsum('cfh,hd->cfd', active, down_weight, precision=highest) + down_bias)
    return validity * (inputs + layer_scale * branch)

def validity_of(group_lengths):
    frame_index = lax.broadcasted_iota(jnp.int32, (group_lengths.shape[0], FRAMES), 1)
    return (frame_index < group_lengths[:, None]).astype(jnp.float32)[:, :, None]

def reference(first_input, second_input, cotangent, lengths, conv_weight, conv_bias, norm_gain, norm_bias, up_weight, up_bias, down_weight, down_bias, layer_scale):
    params = tuple((weight_item.astype(jnp.float32) for weight_item in (conv_weight, conv_bias, norm_gain, norm_bias, up_weight, up_bias, down_weight, down_bias, layer_scale)))
    group_count = CLIPS // 16

    def split(array):
        return array.reshape((group_count, CLIPS // group_count) + array.shape[1:])
    firsts = split(first_input.astype(jnp.float32))
    seconds = split(second_input.astype(jnp.float32))
    cotangents = split(cotangent.astype(jnp.float32))
    group_lengths = split(lengths)

    def first_group(pair):
        inputs, these_lengths = pair
        return forward(inputs, validity_of(these_lengths), params).astype(jnp.bfloat16)
    first_output = lax.map(first_group, (firsts, group_lengths)).reshape(CLIPS, FRAMES, D)

    def second_group(totals, triple):
        inputs, group_cotangent, these_lengths = triple
        validity = validity_of(these_lengths)
        outputs, pullback = jax.vjp(lambda values, weights: forward(values, validity, weights), inputs, params)
        grad_inputs, weight_grads = pullback(group_cotangent)
        totals = jax.tree.map(lambda a, b: a + b, totals, weight_grads)
        return (totals, (outputs.astype(jnp.bfloat16), grad_inputs.astype(jnp.bfloat16)))
    zeros = tuple((jnp.zeros_like(weight_item) for weight_item in params))
    totals, (second_output, input_grad) = lax.scan(second_group, zeros, (seconds, cotangents, group_lengths))
    second_output = second_output.reshape(CLIPS, FRAMES, D)
    input_grad = input_grad.reshape(CLIPS, FRAMES, D)
    return (first_output, second_output, input_grad, totals[0], totals[1], totals[2], totals[3], totals[4], totals[5], totals[6], totals[7], totals[8])
```

```python
import functools
import math

import jax
import jax.numpy as jnp
from jax import lax
from jax.experimental import pallas as pl
from jax.experimental.pallas import tpu as pltpu
from jax.sharding import Mesh
from jax.sharding import PartitionSpec as P

bf16, f32 = jnp.bfloat16, jnp.float32
AXES = ("wide", "half", "core")
CHIPS = ("wide", "half")
ROOT = math.sqrt(0.5)
LANES = 128
HALO = 8
TAIL = 32
SMALL = 16
VMEM = 60 * 2**20
BLOCK = 4

TAPS = 7
CONV_BIAS, GAIN, SHIFT, DOWN_BIAS, SCALE, UP_BIAS = 7, 8, 9, 10, 11, 12


def dot(a, b, ca=1, cb=0, precision=None):
    return lax.dot_general(
        a, b, (((ca,), (cb,)), ((), ())), precision=precision, preferred_element_type=f32
    )


def whole(shape):
    return pl.BlockSpec(shape, lambda i: (0,) * len(shape))


def smem():
    return pl.BlockSpec(memory_space=pltpu.SMEM)


def tail_mask(frames, length, width):
    row = lax.broadcasted_iota(jnp.int32, (TAIL, width), 0) + (frames - TAIL)
    return row < length


def fill_padded(x_ref, m, length, pad_ref):
    frames = x_ref.shape[1]
    body = frames - TAIL
    keep = tail_mask(frames, length, LANES)
    for c in range(x_ref.shape[2] // LANES):
        cs = slice(c * LANES, (c + 1) * LANES)
        x = x_ref[m, :, cs].astype(f32)
        pad_ref[m, c, HALO : HALO + body] = x[:body]
        pad_ref[m, c, HALO + body : HALO + frames] = jnp.where(keep, x[body:], 0.0)


def clear_halo(pad_ref, frames):
    zeros = jnp.zeros(pad_ref.shape[:2] + (HALO, LANES), f32)
    pad_ref[:, :, :HALO] = zeros
    pad_ref[:, :, HALO + frames :] = zeros


def conv_norm(pad_ref, m, small_ref, frames):
    parts = []
    for c in range(pad_ref.shape[1]):
        cs = slice(c * LANES, (c + 1) * LANES)
        acc = small_ref[CONV_BIAS : CONV_BIAS + 1, cs]
        for k in range(TAPS):
            start = HALO + k - TAPS // 2
            acc = acc + small_ref[k : k + 1, cs] * pad_ref[m, c, start : start + frames]
        parts.append(acc)
    conv = jnp.concatenate(parts, axis=1)
    centred = conv - jnp.mean(conv, axis=-1, keepdims=True)
    rstd = lax.rsqrt(jnp.mean(centred * centred, axis=-1, keepdims=True) + 1e-06)
    return (centred * rstd).astype(bf16), rstd


def store_output(out_ref, m, length, x_ref, branch):
    frames = x_ref.shape[1]
    body = frames - TAIL
    keep = tail_mask(frames, length, x_ref.shape[2])
    value = x_ref[m].astype(f32) + branch
    out_ref[m, :body] = value[:body].astype(bf16)
    out_ref[m, body:] = jnp.where(keep, value[body:], 0.0).astype(bf16)


def store_masked(dst_ref, m, length, src_ref):
    frames = src_ref.shape[1]
    body = frames - TAIL
    keep = tail_mask(frames, length, src_ref.shape[2])
    at = m * frames
    dst_ref[at : at + body] = src_ref[m, :body]
    dst_ref[at + body : at + frames] = jnp.where(keep, src_ref[m, body:].astype(f32), 0.0).astype(bf16)


def second_forward(
    len_ref, owner_ref, x_ref, cot_ref, *refs
):
    count = len(refs) - 15
    block_refs = [ref.at[j] for ref in refs[:count] for j in range(ref.shape[0])]
    second_forward_body(len_ref, owner_ref, x_ref, cot_ref, block_refs, *refs[count:])


def second_forward_body(
    len_ref, owner_ref, x_ref, cot_ref, block_refs,
    out_ref, xhat_ref, slope_ref, rstd_ref, up_ref, down_ref, small_ref, bias_ref, gdown_ref, rows_ref,
    pad_ref, act_ref, mcot_ref, acc_ref, csum_ref,
):
    step = pl.program_id(0)
    clips, frames, width = x_ref.shape
    hidden = up_ref.shape[1]
    parts = hidden // width

    @pl.when(step == 0)
    def _():
        devices = len(block_refs)
        up_rows, down_rows = width // devices, hidden // devices
        clear_halo(pad_ref, frames)
        small = jnp.zeros((SMALL, width), f32)
        for ref in block_refs:
            small = small + ref[2 * down_rows :].astype(f32)
        small_ref[...] = small
        scale = small[SCALE : SCALE + 1] * ROOT
        for j, ref in enumerate(block_refs):
            owner = owner_ref[j]
            at = pl.multiple_of(owner * up_rows, up_rows)
            for p in range(parts):
                up_ref[pl.ds(at, up_rows), p * width : (p + 1) * width] = ref[p * up_rows : (p + 1) * up_rows]
            at = pl.multiple_of(owner * down_rows, down_rows)
            down_ref[pl.ds(at, down_rows)] = (ref[down_rows : 2 * down_rows].astype(f32) * scale).astype(bf16)
        ratio = small[SHIFT : SHIFT + 1] / small[GAIN : GAIN + 1]
        shift = dot(
            jnp.broadcast_to(ratio, (8, width)), up_ref[...].astype(f32), precision=lax.Precision.HIGHEST
        )
        for p in range(parts):
            cs = slice(p * width, (p + 1) * width)
            bias_ref[:, cs] = shift[:, cs] + small[UP_BIAS + p : UP_BIAS + p + 1] * ROOT
        acc_ref[...] = jnp.zeros_like(acc_ref)
        csum_ref[...] = jnp.zeros_like(csum_ref)

    lengths = [len_ref[step * clips + m] for m in range(clips)]
    for m in range(clips):
        fill_padded(x_ref, m, lengths[m], pad_ref)
        xhat, rstd = conv_norm(pad_ref, m, small_ref, frames)
        xhat_ref[m * frames : (m + 1) * frames] = xhat
        rstd_ref[m * frames : (m + 1) * frames] = jnp.broadcast_to(rstd, (frames, LANES))
        store_masked(mcot_ref, m, lengths[m], cot_ref)

    xhat = xhat_ref[...]
    for p in range(parts):
        cs = slice(p * width, (p + 1) * width)
        u = dot(xhat, up_ref[:, cs]) + bias_ref[0:1, cs]
        s = 1.0 + lax.erf(u)
        act_ref[:, cs] = (u * s).astype(bf16)
        bell = jnp.exp2(u * u * (-math.log2(math.e)))
        slope_ref[:, cs] = (s + u * bell * (2.0 / math.sqrt(math.pi))).astype(bf16)

    down_bias = small_ref[DOWN_BIAS : DOWN_BIAS + 1] * small_ref[SCALE : SCALE + 1]
    branch = dot(act_ref[...], down_ref[...]) + down_bias
    for m in range(clips):
        store_output(out_ref, m, lengths[m], x_ref, branch[m * frames : (m + 1) * frames])

    mcot = mcot_ref[...]
    acc_ref[...] += dot(act_ref[...], mcot, 0, 0)
    csum_ref[...] += jnp.sum(mcot.astype(f32).reshape(-1, 8, width), axis=0)

    @pl.when(step == pl.num_programs(0) - 1)
    def _():
        total = acc_ref[...]
        gdown_ref[...] = total.astype(bf16)
        scale = small_ref[SCALE : SCALE + 1]
        csum = jnp.sum(csum_ref[...], axis=0, keepdims=True)
        cross = jnp.sum(total * down_ref[...].astype(f32), axis=0, keepdims=True)
        rows_ref[0:1] = csum * scale
        rows_ref[1:2] = cross / scale + csum * small_ref[DOWN_BIAS : DOWN_BIAS + 1]
        rows_ref[2:8] = jnp.zeros((6, width), f32)


def second_backward(
    packed, len_ref, core_ref, cot_ref, x_ref, xhat_ref, slope_ref, rstd_ref, up_ref, down_ref, small_ref, down_rows_ref, _,
    grad_ref, out_a_ref, out_b_ref,
    pad_ref, gh_ref, mcot_ref, acc_ref, hsum_ref, tsum_ref,
):
    step = pl.program_id(0)
    clips, frames, width = x_ref.shape
    hidden = up_ref.shape[1]
    parts = hidden // width

    @pl.when(step == 0)
    def _():
        clear_halo(pad_ref, frames)
        acc_ref[...] = jnp.zeros_like(acc_ref)
        hsum_ref[...] = jnp.zeros_like(hsum_ref)
        tsum_ref[...] = jnp.zeros_like(tsum_ref)

    lengths = [len_ref[step * clips + m] for m in range(clips)]
    for m in range(clips):
        store_masked(mcot_ref, m, lengths[m], cot_ref)
    mcot = mcot_ref[...]
    for p in range(parts):
        cs = slice(p * width, (p + 1) * width)
        ga = dot(mcot, down_ref[cs, :], 1, 1)
        gh = ga * slope_ref[:, cs].astype(f32)
        hsum_ref[:, cs] += jnp.sum(gh.reshape(-1, 8, width), axis=0)
        gh_ref[:, cs] = gh.astype(bf16)
    acc_ref[...] += dot(xhat_ref[...], gh_ref[...], 0, 0)
    g = dot(gh_ref[...], up_ref[...], 1, 1)
    for m in range(clips):
        rows = slice(m * frames, (m + 1) * frames)
        gm = g[rows]
        xhat = xhat_ref[rows].astype(f32)
        mean = jnp.mean(gm, axis=-1, keepdims=True)
        proj = jnp.mean(gm * xhat, axis=-1, keepdims=True)
        rstd = rstd_ref[rows]
        for c in range(width // LANES):
            cs = slice(c * LANES, (c + 1) * LANES)
            gc = (gm[:, cs] - mean - xhat[:, cs] * proj) * rstd
            pad_ref[m, c, HALO : HALO + frames] = gc
            tsum_ref[TAPS, :, cs] += jnp.sum(gc.reshape(-1, 8, LANES), axis=0)
    body = frames - TAIL
    for m in range(clips):
        keep = tail_mask(frames, lengths[m], LANES)
        for c in range(width // LANES):
            cs = slice(c * LANES, (c + 1) * LANES)
            x = x_ref[m, :, cs].astype(f32)
            x = jnp.concatenate([x[:body], jnp.where(keep, x[body:], 0.0)], axis=0)
            total = cot_ref[m, :, cs].astype(f32)
            for k in range(TAPS):
                start = HALO + TAPS // 2 - k
                gc = pad_ref[m, c, start : start + frames]
                total = total + small_ref[k : k + 1, cs] * gc
                tsum_ref[k, :, cs] += jnp.sum((gc * x).reshape(-1, 8, LANES), axis=0)
            grad_ref[m, :body, cs] = total[:body].astype(bf16)
            grad_ref[m, body:, cs] = jnp.where(keep, total[body:], 0.0).astype(bf16)

    @pl.when(step == pl.num_programs(0) - 1)
    def _():
        total = acc_ref[...]
        hsum = jnp.sum(hsum_ref[...], axis=0, keepdims=True)
        columns = small_ref[...].T
        gain, shift = columns[:, GAIN : GAIN + 1], columns[:, SHIFT : SHIFT + 1]
        total_up = (gain * total + shift * hsum) * ROOT
        up = up_ref[...].astype(f32)
        ones = jnp.ones((8, hidden), f32)
        exact = lax.Precision.HIGHEST
        inverse = 1.0 / small_ref[GAIN : GAIN + 1]
        rows = [jnp.sum(tsum_ref[k], axis=0, keepdims=True) for k in range(TAPS + 1)]
        rows.append(dot(ones, up * total, 1, 1, exact)[:1] * inverse)
        rows.append(dot(jnp.broadcast_to(hsum, (8, hidden)), up, 1, 1, exact)[:1] * inverse)
        rows.append(down_rows_ref[0:2])
        if not packed:
            out_a_ref[...] = total_up.astype(bf16)
            rows += [hsum[:, p * width : (p + 1) * width] * ROOT for p in range(parts)]
            rows.append(jnp.zeros((SMALL - UP_BIAS - parts, width), f32))
            out_b_ref[...] = jnp.concatenate(rows, axis=0)
            return
        rows.append(jnp.zeros((SMALL - UP_BIAS, width), f32))
        rows = jnp.concatenate(rows, axis=0)
        bias = hsum * ROOT
        lane = lax.broadcasted_iota(jnp.int32, (SMALL, LANES), 1)
        line = lax.broadcasted_iota(jnp.int32, (SMALL, LANES), 0)
        devices = width // 16
        for owner in range(devices):
            ref = out_a_ref if owner % 2 == 0 else out_b_ref
            for c in range(hidden // LANES):
                ref[owner // 2, c * 16 : (c + 1) * 16] = total_up[
                    owner * 16 : (owner + 1) * 16, c * LANES : (c + 1) * LANES
                ].astype(bf16)
            at = owner * 16 // LANES * LANES
            mine = pltpu.roll(rows[:, at : at + LANES], (LANES - owner * 16 % LANES) % LANES, 1)
            for r in range(parts):
                first = owner * 16 * parts + r * 16
                at = first // LANES * LANES
                part = pltpu.roll(
                    jnp.broadcast_to(bias[:, at : at + LANES], (SMALL, LANES)), (LANES - first % LANES) % LANES, 1
                )
                mine = jnp.where(line == UP_BIAS + r, part, mine)
            high = mine.astype(bf16).astype(f32)
            low = pltpu.roll(mine - high, LANES // 2, 1)
            mine = jnp.where(lane < 16, high, jnp.where((lane >= LANES // 2) & (lane < LANES // 2 + 16), low, 0.0))
            ref[owner // 2, hidden // LANES * 16 :] = mine.astype(bf16)


def first_forward(len_ref, x_ref, up_ref, down_ref, small_ref, bias_ref, _, out_ref, pad_ref, xhat_ref, act_ref):
    step = pl.program_id(0)
    clips, frames, width = x_ref.shape
    parts = up_ref.shape[1] // width

    @pl.when(step == 0)
    def _():
        clear_halo(pad_ref, frames)

    lengths = [len_ref[step * clips + m] for m in range(clips)]
    for m in range(clips):
        fill_padded(x_ref, m, lengths[m], pad_ref)
        xhat_ref[m * frames : (m + 1) * frames] = conv_norm(pad_ref, m, small_ref, frames)[0]
    xhat = xhat_ref[...]
    for p in range(parts):
        cs = slice(p * width, (p + 1) * width)
        u = dot(xhat, up_ref[:, cs]) + bias_ref[0:1, cs]
        act_ref[:, cs] = (u * (1.0 + lax.erf(u))).astype(bf16)
    down_bias = small_ref[DOWN_BIAS : DOWN_BIAS + 1] * small_ref[SCALE : SCALE + 1]
    branch = dot(act_ref[...], down_ref[...]) + down_bias
    for m in range(clips):
        store_output(out_ref, m, lengths[m], x_ref, branch[m * frames : (m + 1) * frames])


def kernel_call(body, name, args, specs, outs, scratch, steps, flops, elements):
    def size(a):
        return math.prod(a.shape) * jnp.dtype(a.dtype).itemsize

    return pl.pallas_call(
        body,
        grid=(steps,),
        in_specs=specs,
        out_specs=[spec for _, spec in outs],
        out_shape=[shape for shape, _ in outs],
        scratch_shapes=scratch,
        compiler_params=pltpu.CompilerParams(vmem_limit_bytes=VMEM),
        cost_estimate=pl.CostEstimate(
            flops=flops,
            bytes_accessed=sum(map(size, args)) + sum(size(s) for s, _ in outs),
            transcendentals=elements,
        ),
        name=name,
    )(*args)


def shape(dims, dtype):
    return jax.ShapeDtypeStruct(dims, dtype)


def own_block(
    me_ref, conv_ref, conv_bias_ref, gain_ref, shift_ref, up_ref, up_bias_ref, down_ref, down_bias_ref, scale_ref,
    block_ref,
    row_ref,
):
    own, hidden = up_ref.shape
    rows, width = down_ref.shape
    parts = hidden // width
    me = me_ref[0]
    i = lax.broadcasted_iota(jnp.int32, (own, own), 0)
    j = lax.broadcasted_iota(jnp.int32, (own, own), 1)
    scaled = dot(jnp.where(i == j, gain_ref[...].astype(f32), 0.0).astype(bf16), up_ref[...]) * ROOT
    for p in range(parts):
        block_ref[p * own : (p + 1) * own] = scaled[:, p * width : (p + 1) * width].astype(bf16)
    block_ref[rows : 2 * rows] = down_ref[...]
    vectors = [r[...].astype(f32) for r in (conv_bias_ref, gain_ref, shift_ref, down_bias_ref, scale_ref)]
    small = jnp.concatenate([conv_ref[...].astype(f32)] + vectors + [jnp.zeros((SMALL - UP_BIAS, own), f32)], axis=0)
    small = jnp.concatenate([small, jnp.zeros((SMALL, LANES - own), f32)], axis=1)
    row_ref[...] = jnp.zeros_like(row_ref)
    per = LANES // own
    at = pl.multiple_of(me // per * LANES, LANES)
    row_ref[:, pl.ds(at, LANES)] = pltpu.roll(small, me % per * own, 1)
    bias = jnp.concatenate([up_bias_ref[...].astype(f32), jnp.zeros((1, 2 * LANES - rows), f32)], axis=1)
    bias = pltpu.roll(jnp.broadcast_to(bias, (8, 2 * LANES)), me * rows % LANES, 1)
    first = me * rows // LANES
    tiles = width // LANES
    for t in range(hidden // LANES):
        part = jnp.where(first == t, bias[:1, :LANES], jnp.where(first + 1 == t, bias[:1, LANES:], 0.0))
        row_ref[UP_BIAS + t // tiles : UP_BIAS + t // tiles + 1, t % tiles * LANES : (t % tiles + 1) * LANES] = part

    block_ref[2 * rows :] = row_ref[...].astype(bf16)


def quick(width, hidden, devices):
    return devices == 32 and width == 16 * devices and hidden % width == 0


def flipped(a, bits, devices):
    return lax.ppermute(a, AXES, [(i, i ^ bits) for i in range(devices)])


def gather_weights(weights, devices):
    conv_weight, conv_bias, gain, shift, up, up_bias, down, down_bias, scale = weights
    up_rows, hidden = up.shape
    down_rows, width = down.shape
    parts = hidden // width
    me = lax.axis_index(AXES).astype(jnp.int32)
    if quick(width, hidden, devices):
        row = lambda v: v.reshape(1, -1)
        args = (me.reshape(1), conv_weight, row(conv_bias), row(gain), row(shift), up, row(up_bias), down, row(down_bias), row(scale))
        block = pl.pallas_call(
            own_block,
            in_specs=[smem()] + [pl.BlockSpec(memory_space=pltpu.VMEM)] * 9,
            out_specs=pl.BlockSpec(memory_space=pltpu.VMEM),
            out_shape=shape((2 * down_rows + SMALL, width), bf16),
            scratch_shapes=[pltpu.VMEM((SMALL, width), f32)],
            name="own_block",
        )(*args)
        both = jnp.stack([block, flipped(block, 16, devices)])
        have = {0: both}
        for flip, start in ((8, 0), (4, 0), (2, 0), (2, 4), (8, 2), (4, 8), (8, 6)):
            have[flip ^ start] = flipped(have[start], flip, devices)
        for start in list(have):
            have[start ^ 1] = flipped(have[start], 1, devices)
        order = [start ^ far for start in have for far in (0, 16)]
        return list(have.values()), me ^ jnp.array(order, jnp.int32)
    everyone = lambda a, axis: lax.all_gather(a, AXES, axis=axis, tiled=True)
    up = (up.astype(f32) * gain.astype(f32)[:, None] * ROOT).astype(bf16)
    up, down, up_bias = everyone(up, 0), everyone(down, 0), everyone(up_bias, 0)
    vectors = jnp.stack([conv_bias, gain, shift, down_bias, scale])
    small = jnp.concatenate([everyone(conv_weight, 1), everyone(vectors, 1), up_bias.reshape(parts, width)], axis=0)
    small = jnp.pad(small, ((0, SMALL - small.shape[0]), (0, 0)))
    count = width // 16
    up = up.reshape(count, 16, parts, width).swapaxes(1, 2).reshape(count, 16 * parts, width)
    down = down.reshape(count, 16 * parts, width)
    small = jnp.pad(small[None], ((0, count - 1), (0, 0), (0, 0)))
    return [jnp.concatenate([up, down, small], axis=1)], jnp.arange(count, dtype=jnp.int32)


def add_pair(keep_ref, got_ref, _, out_ref):
    out_ref[...] = (keep_ref[...].astype(f32) + got_ref[...].astype(f32)).astype(bf16)


def pair_sum(keep, got, after):
    half = keep.shape[0] // 2
    spec = pl.BlockSpec((half,) + keep.shape[1:], lambda i: (i, 0, 0))
    return pl.pallas_call(
        add_pair,
        grid=(2,),
        in_specs=[spec, spec, pl.BlockSpec(memory_space=pl.ANY)],
        out_specs=spec,
        out_shape=shape(keep.shape, bf16),
        name="add_pair",
    )(keep, got, after)


def finish(down_ref, up_ref, small_ref, grad_down_ref, grad_up_ref, rows_ref):
    total = jnp.zeros(down_ref.shape[1:], f32)
    for j in range(down_ref.shape[0]):
        total = total + down_ref[j].astype(f32)
    grad_down_ref[...] = total * (small_ref[SCALE : SCALE + 1] * ROOT)
    total = jnp.zeros(up_ref.shape[1:], f32)
    for j in range(up_ref.shape[0]):
        total = total + up_ref[j].astype(f32)
    own, hidden = grad_up_ref.shape
    for c in range(hidden // LANES):
        grad_up_ref[:, c * LANES : (c + 1) * LANES] = total[c * own : (c + 1) * own]
    rest = total[hidden // LANES * own :]
    rows_ref[...] = rest + pltpu.roll(rest, LANES // 2, 1)


def on_device(chips, first_input, second_input, cotangent, lengths, *weights):
    clips, frames, width = second_input.shape
    hidden = weights[6].shape[0] * chips * 2
    tokens = clips * frames
    block = math.gcd(clips, BLOCK)
    steps = clips // block
    rows = block * frames
    core = lax.axis_index("core").astype(jnp.int32)
    matmul = 2 * tokens * width * hidden

    blocks, owners = gather_weights(weights, chips * 2)

    clip_spec = pl.BlockSpec((block, frames, width), lambda i: (i, 0, 0))
    row_spec = lambda n: pl.BlockSpec((rows, n), lambda i: (i, 0))
    clip_out = (shape(second_input.shape, bf16), clip_spec)
    pad = pltpu.VMEM((block, width // LANES, frames + 2 * HALO, LANES), f32)

    second_output, xhat, slope, rstd, up, down, small, bias, gdown, down_grad_rows = kernel_call(
        second_forward,
        "second_forward",
        (lengths, owners, second_input, cotangent, *blocks),
        [smem(), smem(), clip_spec, clip_spec] + [whole(b.shape) for b in blocks],
        [
            clip_out,
            (shape((tokens, width), bf16), row_spec(width)),
            (shape((tokens, hidden), bf16), row_spec(hidden)),
            (shape((tokens, LANES), f32), row_spec(LANES)),
            (shape((width, hidden), bf16), whole((width, hidden))),
            (shape((hidden, width), bf16), whole((hidden, width))),
            (shape((SMALL, width), f32), whole((SMALL, width))),
            (shape((8, hidden), f32), whole((8, hidden))),
            (shape((hidden, width), bf16), whole((hidden, width))),
            (shape((8, width), f32), whole((8, width))),
        ],
        [
            pad,
            pltpu.VMEM((rows, hidden), bf16),
            pltpu.VMEM((rows, width), bf16),
            pltpu.VMEM((hidden, width), f32),
            pltpu.VMEM((8, width), f32),
        ],
        steps,
        3 * matmul,
        2 * tokens * hidden,
    )

    devices = chips * 2
    fast = quick(width, hidden, devices)
    if fast:
        gdown_parts = lax.all_to_all(gdown.reshape(devices, hidden // devices, width), AXES, 0, 0, tiled=True)
        payload = shape((chips, hidden // LANES * 16 + SMALL, LANES), bf16)
        outs = [(payload, whole(payload.shape))] * 2
    else:
        outs = [
            (shape((width, hidden), bf16), whole((width, hidden))),
            (shape((SMALL, width), f32), whole((SMALL, width))),
        ]

    input_grad, out_a, out_b = kernel_call(
        functools.partial(second_backward, fast),
        "second_backward",
        (lengths, core.reshape(1), cotangent, second_input, xhat, slope, rstd, up, down, small, down_grad_rows, gdown),
        [
            smem(), smem(), clip_spec, clip_spec, row_spec(width), row_spec(hidden), row_spec(LANES),
            whole(up.shape), whole(down.shape), whole(small.shape), whole(down_grad_rows.shape),
            pl.BlockSpec(memory_space=pl.ANY),
        ],
        [
            clip_out,
            *outs,
        ],
        [
            pad,
            pltpu.VMEM((rows, hidden), bf16),
            pltpu.VMEM((rows, width), bf16),
            pltpu.VMEM((width, hidden), f32),
            pltpu.VMEM((8, hidden), f32),
            pltpu.VMEM((TAPS + 1, 8, width), f32),
        ],
        steps,
        3 * matmul,
        0,
    )

    if fast:
        keep = jnp.where(core == 0, out_a, out_b)
        got = flipped(jnp.where(core == 0, out_b, out_a), 1, devices)
        gup_pair = pair_sum(keep, got, gdown_parts)
        gup_parts = lax.all_to_all(gup_pair, CHIPS, 0, 0, tiled=True)
    else:
        gup_pair = out_a

    (first_output,) = kernel_call(
        first_forward,
        "first_forward",
        (lengths, first_input, up, down, small, bias, gup_pair),
        [
            smem(), clip_spec, whole(up.shape), whole(down.shape), whole(small.shape), whole(bias.shape),
            pl.BlockSpec(memory_space=pl.ANY),
        ],
        [clip_out],
        [pad, pltpu.VMEM((rows, width), bf16), pltpu.VMEM((rows, hidden), bf16)],
        steps,
        2 * matmul,
        tokens * hidden,
    )

    own = width // devices
    if fast:
        grad_down, grad_up, sums = pl.pallas_call(
            finish,
            out_shape=[shape((hidden // devices, width), f32), shape((own, hidden), f32), shape((SMALL, LANES), f32)],
            name="finish",
        )(gdown_parts, gup_parts, small)
        vector = lambda r: sums[r, :own]
        grad_taps = sums[:TAPS, :own]
        grad_up_bias = sums[UP_BIAS : UP_BIAS + hidden // width, :own].reshape(-1)
    else:
        scatter = lambda a: lax.psum_scatter(a.astype(f32), AXES, scatter_dimension=0, tiled=True)
        me = lax.axis_index(AXES)
        grad_down = scatter(gdown) * (small[SCALE] * ROOT)
        grad_up = scatter(out_a)
        sums = lax.psum(out_b, AXES)
        vector = lambda r: lax.dynamic_slice(sums[r], (me * own,), (own,))
        grad_taps = lax.dynamic_slice(sums, (0, me * own), (TAPS, own))
        grad_up_bias = lax.dynamic_slice(
            sums[UP_BIAS : UP_BIAS + hidden // width].reshape(-1), (me * (hidden // devices),), (hidden // devices,)
        )
    return (
        first_output,
        second_output,
        input_grad,
        grad_taps,
        vector(CONV_BIAS),
        vector(GAIN),
        vector(SHIFT),
        grad_up,
        grad_up_bias,
        grad_down,
        vector(DOWN_BIAS),
        vector(SCALE),
    )


def solution(mesh):
    wide, narrow = mesh.devices.shape
    grid = Mesh(mesh.devices.reshape(wide, narrow // 2, 2), AXES)
    chips = wide * narrow // 2
    rows = P(AXES)
    columns = P(None, AXES)

    def run(*args):
        return on_device(chips, *args)

    return jax.shard_map(
        run,
        mesh=grid,
        in_specs=(rows, rows, rows, rows, columns, rows, rows, rows, rows, rows, rows, rows, rows),
        out_specs=(rows, rows, rows, columns, rows, rows, rows, rows, rows, rows, rows, rows),
        check_vma=False,
    )
```

```python
import functools
import math

import jax
import jax.numpy as jnp
from jax import lax
from jax.experimental import pallas as pl
from jax.experimental.pallas import tpu as pltpu
from jax.sharding import Mesh
from jax.sharding import PartitionSpec as P

bf16, f32 = jnp.bfloat16, jnp.float32
AXES = ("wide", "half", "core")
CHIPS = ("wide", "half")
ROOT = math.sqrt(0.5)
LANES = 128
HALO = 8
TAIL = 32
CHUNK = 16
SMALL = 16
VMEM = 60 * 2**20
BLOCK = 4

TAPS = 7
CONV_BIAS, GAIN, SHIFT, DOWN_BIAS, SCALE, UP_BIAS = 7, 8, 9, 10, 11, 12


def dot(a, b, ca=1, cb=0, precision=None):
    return lax.dot_general(
        a, b, (((ca,), (cb,)), ((), ())), precision=precision, preferred_element_type=f32
    )


def whole(shape):
    return pl.BlockSpec(shape, lambda i: (0,) * len(shape))


def smem():
    return pl.BlockSpec(memory_space=pltpu.SMEM)


def tail_mask(frames, length, width):
    row = lax.broadcasted_iota(jnp.int32, (TAIL, width), 0) + (frames - TAIL)
    return row < length


def fill_padded(x_ref, m, length, pad_ref):
    frames = x_ref.shape[1]
    body = frames - TAIL
    keep = tail_mask(frames, length, LANES)
    for c in range(x_ref.shape[2] // LANES):
        cs = slice(c * LANES, (c + 1) * LANES)
        x = x_ref[m, :, cs].astype(f32)
        pad_ref[m, c, HALO : HALO + body] = x[:body]
        pad_ref[m, c, HALO + body : HALO + frames] = jnp.where(keep, x[body:], 0.0)


def clear_halo(pad_ref, frames):
    zeros = jnp.zeros(pad_ref.shape[:2] + (HALO, LANES), f32)
    pad_ref[:, :, :HALO] = zeros
    pad_ref[:, :, HALO + frames :] = zeros


def conv_norm(pad_ref, m, small_ref, frames):
    parts = []
    for c in range(pad_ref.shape[1]):
        cs = slice(c * LANES, (c + 1) * LANES)
        acc = small_ref[CONV_BIAS : CONV_BIAS + 1, cs]
        for k in range(TAPS):
            start = HALO + k - TAPS // 2
            acc = acc + small_ref[k : k + 1, cs] * pad_ref[m, c, start : start + frames]
        parts.append(acc)
    conv = jnp.concatenate(parts, axis=1)
    centred = conv - jnp.mean(conv, axis=-1, keepdims=True)
    rstd = lax.rsqrt(jnp.mean(centred * centred, axis=-1, keepdims=True) + 1e-06)
    return (centred * rstd).astype(bf16), rstd


def conv_norm_into(pad_ref, m, small_ref, frames, xhat_ref, rstd_ref):
    width = xhat_ref.shape[1]
    for r in range(0, frames, CHUNK):
        parts = []
        for c in range(width // LANES):
            cs = slice(c * LANES, (c + 1) * LANES)
            acc = small_ref[CONV_BIAS : CONV_BIAS + 1, cs]
            for k in range(TAPS):
                start = HALO + k - TAPS // 2 + r
                acc = acc + small_ref[k : k + 1, cs] * pad_ref[m, c, start : start + CHUNK]
            parts.append(acc)
        mean = jnp.sum(sum(parts[1:], parts[0]), axis=-1, keepdims=True) / width
        parts = [p - mean for p in parts]
        square = sum((p * p for p in parts[1:]), parts[0] * parts[0])
        rstd = lax.rsqrt(jnp.sum(square, axis=-1, keepdims=True) / width + 1e-06)
        rows = slice(m * frames + r, m * frames + r + CHUNK)
        rstd_ref[rows] = jnp.broadcast_to(rstd, (CHUNK, LANES))
        for c, p in enumerate(parts):
            xhat_ref[rows, c * LANES : (c + 1) * LANES] = (p * rstd).astype(bf16)


def store_output(out_ref, m, length, x_ref, branch):
    frames = x_ref.shape[1]
    body = frames - TAIL
    keep = tail_mask(frames, length, x_ref.shape[2])
    value = x_ref[m].astype(f32) + branch
    out_ref[m, :body] = value[:body].astype(bf16)
    out_ref[m, body:] = jnp.where(keep, value[body:], 0.0).astype(bf16)


def store_masked(dst_ref, m, length, src_ref):
    frames = src_ref.shape[1]
    body = frames - TAIL
    keep = tail_mask(frames, length, src_ref.shape[2])
    at = m * frames
    dst_ref[at : at + body] = src_ref[m, :body]
    dst_ref[at + body : at + frames] = jnp.where(keep, src_ref[m, body:].astype(f32), 0.0).astype(bf16)


def second_forward(
    owners, len_ref, me_ref, x_ref, next_ref, cot_ref, *refs
):
    count = len(refs) - 17
    block_refs = [ref.at[j] for ref in refs[:count] for j in range(ref.shape[0])]
    second_forward_body(owners, len_ref, me_ref, x_ref, next_ref, cot_ref, block_refs, *refs[count:])


def second_forward_body(
    owners, len_ref, me_ref, x_ref, next_ref, cot_ref, block_refs,
    out_ref, xhat_ref, slope_ref, rstd_ref, up_ref, down_ref, small_ref, bias_ref, gdown_ref, rows_ref,
    pad_ref, act_ref, mcot_ref, acc_ref, csum_ref, xnext_ref, rnext_ref,
):
    step = pl.program_id(0)
    clips, frames, width = x_ref.shape
    hidden = up_ref.shape[1]
    parts = hidden // width

    @pl.when(step == 0)
    def _():
        devices = len(block_refs)
        up_rows, down_rows = width // devices, hidden // devices
        clear_halo(pad_ref, frames)
        small = jnp.zeros((SMALL, width), f32)
        for ref in block_refs:
            small = small + ref[2 * down_rows :].astype(f32)
        small_ref[...] = small
        scale = small[SCALE : SCALE + 1] * ROOT
        for j, ref in enumerate(block_refs):
            owner = me_ref[0] ^ owners[j]
            at = pl.multiple_of(owner * up_rows, up_rows)
            for p in range(parts):
                up_ref[pl.ds(at, up_rows), p * width : (p + 1) * width] = ref[p * up_rows : (p + 1) * up_rows]
            at = pl.multiple_of(owner * down_rows, down_rows)
            down_ref[pl.ds(at, down_rows)] = (ref[down_rows : 2 * down_rows].astype(f32) * scale).astype(bf16)
        columns = small.T
        ratio = columns[:, SHIFT : SHIFT + 1] / columns[:, GAIN : GAIN + 1]
        shift = jnp.sum((up_ref[...].astype(f32) * ratio).reshape(-1, 8, hidden), axis=0)
        shift = jnp.broadcast_to(jnp.sum(shift, axis=0, keepdims=True), (8, hidden))
        for p in range(parts):
            cs = slice(p * width, (p + 1) * width)
            bias_ref[:, cs] = shift[:, cs] + small[UP_BIAS + p : UP_BIAS + p + 1] * ROOT
        acc_ref[...] = jnp.zeros_like(acc_ref)
        csum_ref[...] = jnp.zeros_like(csum_ref)
        for m in range(clips):
            fill_padded(x_ref, m, len_ref[m], pad_ref)
            conv_norm_into(pad_ref, m, small_ref, frames, xnext_ref, rnext_ref)

    lengths = [len_ref[step * clips + m] for m in range(clips)]
    xhat_ref[...] = xnext_ref[...]
    rstd_ref[...] = rnext_ref[...]
    for m in range(clips):
        store_masked(mcot_ref, m, lengths[m], cot_ref)

    for p in range(parts):
        cs = slice(p * width, (p + 1) * width)
        u = dot(xhat_ref[...], up_ref[:, cs]) + bias_ref[0:1, cs]
        s = 1.0 + lax.erf(u)
        act_ref[:, cs] = (u * s).astype(bf16)
        bell = jnp.exp2(u * u * (-math.log2(math.e)))
        slope_ref[:, cs] = (s + u * bell * (2.0 / math.sqrt(math.pi))).astype(bf16)

    down_bias = small_ref[DOWN_BIAS : DOWN_BIAS + 1] * small_ref[SCALE : SCALE + 1]
    branch = dot(act_ref[...], down_ref[...]) + down_bias
    for m in range(clips):
        store_output(out_ref, m, lengths[m], x_ref, branch[m * frames : (m + 1) * frames])

    acc_ref[...] += dot(mcot_ref[...], act_ref[...], 0, 0)
    csum_ref[...] += jnp.sum(mcot_ref[...].astype(f32).reshape(-1, 8, width), axis=0)
    later = jnp.minimum(step + 1, pl.num_programs(0) - 1) * clips
    for m in range(clips):
        fill_padded(next_ref, m, len_ref[later + m], pad_ref)
        conv_norm_into(pad_ref, m, small_ref, frames, xnext_ref, rnext_ref)

    @pl.when(step == pl.num_programs(0) - 1)
    def _():
        total = acc_ref[...].T
        gdown_ref[...] = total.astype(bf16)
        scale = small_ref[SCALE : SCALE + 1]
        csum = jnp.sum(csum_ref[...], axis=0, keepdims=True)
        cross = jnp.sum(total * down_ref[...].astype(f32), axis=0, keepdims=True)
        rows_ref[0:1] = csum * scale
        rows_ref[1:2] = cross / scale + csum * small_ref[DOWN_BIAS : DOWN_BIAS + 1]
        rows_ref[2:8] = jnp.zeros((6, width), f32)


def second_backward(
    packed, len_ref, core_ref, cot_ref, x_ref, xhat_ref, slope_ref, rstd_ref, up_ref, down_ref, small_ref, down_rows_ref, _,
    grad_ref, out_a_ref, out_b_ref,
    pad_ref, gh_ref, mcot_ref, acc_ref, hsum_ref, tsum_ref,
):
    step = pl.program_id(0)
    clips, frames, width = x_ref.shape
    hidden = up_ref.shape[1]
    parts = hidden // width

    @pl.when(step == 0)
    def _():
        clear_halo(pad_ref, frames)
        acc_ref[...] = jnp.zeros_like(acc_ref)
        hsum_ref[...] = jnp.zeros_like(hsum_ref)
        tsum_ref[...] = jnp.zeros_like(tsum_ref)

    lengths = [len_ref[step * clips + m] for m in range(clips)]
    for m in range(clips):
        store_masked(mcot_ref, m, lengths[m], cot_ref)
    for m in range(clips):
        rows = slice(m * frames, (m + 1) * frames)
        for p in range(parts):
            cs = slice(p * width, (p + 1) * width)
            ga = dot(mcot_ref[rows], down_ref[cs, :], 1, 1)
            gh = ga * slope_ref[rows, cs].astype(f32)
            hsum_ref[:, cs] += jnp.sum(gh.reshape(-1, 8, width), axis=0)
            gh_ref[rows, cs] = gh.astype(bf16)
    for m in range(clips):
        rows = slice(m * frames, (m + 1) * frames)
        g = dot(gh_ref[rows], up_ref[...], 1, 1)
        xhat = xhat_ref[rows].astype(f32)
        mean = jnp.mean(g, axis=-1, keepdims=True)
        proj = jnp.mean(g * xhat, axis=-1, keepdims=True)
        rstd = rstd_ref[rows]
        for c in range(width // LANES):
            cs = slice(c * LANES, (c + 1) * LANES)
            gc = (g[:, cs] - mean - xhat[:, cs] * proj) * rstd
            pad_ref[m, c, HALO : HALO + frames] = gc
            tsum_ref[TAPS, :, cs] += jnp.sum(gc.reshape(-1, 8, LANES), axis=0)
    acc_ref[...] += dot(xhat_ref[...], gh_ref[...], 0, 0)
    for m in range(clips):
        keep = tail_mask(frames, lengths[m], LANES)
        for c in range(width // LANES):
            cs = slice(c * LANES, (c + 1) * LANES)
            sums = [jnp.zeros((8, LANES), f32)] * TAPS
            for r in range(0, frames, TAIL):
                x = x_ref[m, r : r + TAIL, cs].astype(f32)
                total = cot_ref[m, r : r + TAIL, cs].astype(f32)
                if r + TAIL == frames:
                    x = jnp.where(keep, x, 0.0)
                for k in range(TAPS):
                    start = HALO + TAPS // 2 - k + r
                    gc = pad_ref[m, c, start : start + TAIL]
                    total = total + small_ref[k : k + 1, cs] * gc
                    sums[k] = sums[k] + jnp.sum((gc * x).reshape(-1, 8, LANES), axis=0)
                if r + TAIL == frames:
                    total = jnp.where(keep, total, 0.0)
                grad_ref[m, r : r + TAIL, cs] = total.astype(bf16)
            for k in range(TAPS):
                tsum_ref[k, :, cs] += sums[k]

    @pl.when(step == pl.num_programs(0) - 1)
    def _():
        total = acc_ref[...]
        hsum = jnp.sum(hsum_ref[...], axis=0, keepdims=True)
        columns = small_ref[...].T
        gain, shift = columns[:, GAIN : GAIN + 1] * ROOT, columns[:, SHIFT : SHIFT + 1] * ROOT
        inverse = 1.0 / small_ref[GAIN : GAIN + 1]
        rows = [jnp.sum(tsum_ref[k], axis=0, keepdims=True) for k in range(TAPS + 1)]
        up = up_ref[...].astype(f32)
        for value in (up * total, up * hsum):
            part = value[:, :LANES]
            for c in range(1, hidden // LANES):
                part = part + value[:, c * LANES : (c + 1) * LANES]
            rows.append(jnp.sum(part.T, axis=0, keepdims=True) * inverse)
        rows.append(down_rows_ref[0:2])
        if not packed:
            out_a_ref[...] = (gain * total + shift * hsum).astype(bf16)
            rows += [hsum[:, p * width : (p + 1) * width] * ROOT for p in range(parts)]
            rows.append(jnp.zeros((SMALL - UP_BIAS - parts, width), f32))
            out_b_ref[...] = jnp.concatenate(rows, axis=0)
            return
        rows.append(jnp.zeros((SMALL - UP_BIAS, width), f32))
        rows = jnp.concatenate(rows, axis=0)
        bias = hsum * ROOT
        lane = lax.broadcasted_iota(jnp.int32, (SMALL, LANES), 1)
        line = lax.broadcasted_iota(jnp.int32, (SMALL, LANES), 0)
        devices = width // 16
        even = core_ref[0] == 0
        acc_ref[...] = gain * total + shift * hsum
        for chip in range(devices // 2):
            for ref, core in ((out_a_ref, core_ref[0]), (out_b_ref, 1 - core_ref[0])):
                at = pl.multiple_of(chip * 32 + core * 16, 16)
                for c in range(hidden // LANES):
                    value = acc_ref[pl.ds(at, 16), c * LANES : (c + 1) * LANES]
                    ref[chip, c * 16 : (c + 1) * 16] = value.astype(bf16)
        pair = []
        for owner in range(devices):
            at = owner * 16 // LANES * LANES
            mine = pltpu.roll(rows[:, at : at + LANES], (LANES - owner * 16 % LANES) % LANES, 1)
            for r in range(parts):
                first = owner * 16 * parts + r * 16
                at = first // LANES * LANES
                part = pltpu.roll(
                    jnp.broadcast_to(bias[:, at : at + LANES], (SMALL, LANES)), (LANES - first % LANES) % LANES, 1
                )
                mine = jnp.where(line == UP_BIAS + r, part, mine)
            high = mine.astype(bf16).astype(f32)
            low = pltpu.roll(mine - high, LANES // 2, 1)
            pair.append(jnp.where(lane < 16, high, jnp.where((lane >= LANES // 2) & (lane < LANES // 2 + 16), low, 0.0)))
            if owner % 2:
                first, second = pair[-2:]
                out_a_ref[owner // 2, hidden // LANES * 16 :] = jnp.where(even, first, second).astype(bf16)
                out_b_ref[owner // 2, hidden // LANES * 16 :] = jnp.where(even, second, first).astype(bf16)


def first_forward(
    len_ref, x_ref, up_ref, down_ref, small_ref, bias_ref, _, parts_ref, scale_ref,
    out_ref, grad_down_ref,
    pad_ref, xhat_ref, act_ref,
):
    total = jnp.zeros(parts_ref.shape[1:], f32)
    for j in range(parts_ref.shape[0]):
        total = total + parts_ref[j].astype(f32)
    grad_down_ref[...] = total * (scale_ref[SCALE : SCALE + 1] * ROOT)

    step = pl.program_id(0)
    clips, frames, width = x_ref.shape
    parts = up_ref.shape[1] // width

    @pl.when(step == 0)
    def _():
        clear_halo(pad_ref, frames)

    lengths = [len_ref[step * clips + m] for m in range(clips)]
    down_bias = small_ref[DOWN_BIAS : DOWN_BIAS + 1] * small_ref[SCALE : SCALE + 1]

    def front(m):
        fill_padded(x_ref, m, lengths[m], pad_ref)
        xhat_ref[m * frames : (m + 1) * frames] = conv_norm(pad_ref, m, small_ref, frames)[0]

    front(0)
    for m in range(clips):
        if m + 1 < clips:
            front(m + 1)
        rows = slice(m * frames, (m + 1) * frames)
        for p in range(2 * parts):
            cs = slice(p * width // 2, (p + 1) * width // 2)
            u = dot(xhat_ref[rows], up_ref[:, cs]) + bias_ref[0:1, cs]
            act_ref[rows, cs] = (u * (1.0 + lax.erf(u))).astype(bf16)
        store_output(out_ref, m, lengths[m], x_ref, dot(act_ref[rows], down_ref[...]) + down_bias)


def kernel_call(body, name, args, specs, outs, scratch, steps, flops, elements):
    def size(a):
        return math.prod(a.shape) * jnp.dtype(a.dtype).itemsize

    return pl.pallas_call(
        body,
        grid=(steps,),
        in_specs=specs,
        out_specs=[spec for _, spec in outs],
        out_shape=[shape for shape, _ in outs],
        scratch_shapes=scratch,
        compiler_params=pltpu.CompilerParams(vmem_limit_bytes=VMEM),
        cost_estimate=pl.CostEstimate(
            flops=flops,
            bytes_accessed=sum(map(size, args)) + sum(size(s) for s, _ in outs),
            transcendentals=elements,
        ),
        name=name,
    )(*args)


def shape(dims, dtype):
    return jax.ShapeDtypeStruct(dims, dtype)


def own_block(
    me_ref, conv_ref, conv_bias_ref, gain_ref, shift_ref, up_ref, up_bias_ref, down_ref, down_bias_ref, scale_ref,
    block_ref,
    row_ref,
):
    own, hidden = up_ref.shape
    rows, width = down_ref.shape
    parts = hidden // width
    me = me_ref[0]
    i = lax.broadcasted_iota(jnp.int32, (own, own), 0)
    j = lax.broadcasted_iota(jnp.int32, (own, own), 1)
    scaled = dot(jnp.where(i == j, gain_ref[...].astype(f32), 0.0).astype(bf16), up_ref[...]) * ROOT
    for p in range(parts):
        block_ref[p * own : (p + 1) * own] = scaled[:, p * width : (p + 1) * width].astype(bf16)
    block_ref[rows : 2 * rows] = down_ref[...]
    vectors = [r[...].astype(f32) for r in (conv_bias_ref, gain_ref, shift_ref, down_bias_ref, scale_ref)]
    small = jnp.concatenate([conv_ref[...].astype(f32)] + vectors + [jnp.zeros((SMALL - UP_BIAS, own), f32)], axis=0)
    small = jnp.concatenate([small, jnp.zeros((SMALL, LANES - own), f32)], axis=1)
    row_ref[...] = jnp.zeros_like(row_ref)
    per = LANES // own
    at = pl.multiple_of(me // per * LANES, LANES)
    row_ref[:, pl.ds(at, LANES)] = pltpu.roll(small, me % per * own, 1)
    bias = jnp.concatenate([up_bias_ref[...].astype(f32), jnp.zeros((1, 2 * LANES - rows), f32)], axis=1)
    bias = pltpu.roll(jnp.broadcast_to(bias, (8, 2 * LANES)), me * rows % LANES, 1)
    first = me * rows // LANES
    tiles = width // LANES
    for t in range(hidden // LANES):
        part = jnp.where(first == t, bias[:1, :LANES], jnp.where(first + 1 == t, bias[:1, LANES:], 0.0))
        row_ref[UP_BIAS + t // tiles : UP_BIAS + t // tiles + 1, t % tiles * LANES : (t % tiles + 1) * LANES] = part

    block_ref[2 * rows :] = row_ref[...].astype(bf16)


def quick(width, hidden, devices):
    return devices == 32 and width == 16 * devices and hidden % width == 0


def flipped(a, bits, devices):
    return lax.ppermute(a, AXES, [(i, i ^ bits) for i in range(devices)])


def gather_weights(weights, devices):
    conv_weight, conv_bias, gain, shift, up, up_bias, down, down_bias, scale = weights
    up_rows, hidden = up.shape
    down_rows, width = down.shape
    parts = hidden // width
    me = lax.axis_index(AXES).astype(jnp.int32)
    if quick(width, hidden, devices):
        row = lambda v: v.reshape(1, -1)
        args = (me.reshape(1), conv_weight, row(conv_bias), row(gain), row(shift), up, row(up_bias), down, row(down_bias), row(scale))
        block = pl.pallas_call(
            own_block,
            in_specs=[smem()] + [pl.BlockSpec(memory_space=pltpu.VMEM)] * 9,
            out_specs=pl.BlockSpec(memory_space=pltpu.VMEM),
            out_shape=shape((2 * down_rows + SMALL, width), bf16),
            scratch_shapes=[pltpu.VMEM((SMALL, width), f32)],
            name="own_block",
        )(*args)
        both = jnp.stack([block, flipped(block, 16, devices)])
        have = {0: both}
        for flip, start in ((8, 0), (4, 0), (2, 0), (2, 4), (8, 2), (4, 8), (8, 6)):
            have[flip ^ start] = flipped(have[start], flip, devices)
        for start in list(have):
            have[start ^ 1] = flipped(have[start], 1, devices)
        order = [start ^ far for start in have for far in (0, 16)]
        return list(have.values()), order, me.reshape(1)
    everyone = lambda a, axis: lax.all_gather(a, AXES, axis=axis, tiled=True)
    up = (up.astype(f32) * gain.astype(f32)[:, None] * ROOT).astype(bf16)
    up, down, up_bias = everyone(up, 0), everyone(down, 0), everyone(up_bias, 0)
    vectors = jnp.stack([conv_bias, gain, shift, down_bias, scale])
    small = jnp.concatenate([everyone(conv_weight, 1), everyone(vectors, 1), up_bias.reshape(parts, width)], axis=0)
    small = jnp.pad(small, ((0, SMALL - small.shape[0]), (0, 0)))
    count = width // 16
    up = up.reshape(count, 16, parts, width).swapaxes(1, 2).reshape(count, 16 * parts, width)
    down = down.reshape(count, 16 * parts, width)
    small = jnp.pad(small[None], ((0, count - 1), (0, 0), (0, 0)))
    return [jnp.concatenate([up, down, small], axis=1)], list(range(count)), jnp.zeros((1,), jnp.int32)


def finish(parts_ref, grad_up_ref, taps_ref, up_bias_ref, *vector_refs):
    total = jnp.zeros(parts_ref.shape[1:], f32)
    for j in range(parts_ref.shape[0]):
        total = total + parts_ref[j].astype(f32)
    own, hidden = grad_up_ref.shape
    for c in range(hidden // LANES):
        grad_up_ref[:, c * LANES : (c + 1) * LANES] = total[c * own : (c + 1) * own]
    rows = total[hidden // LANES * own :]
    rows = rows + pltpu.roll(rows, LANES // 2, 1)
    taps_ref[...] = rows[:TAPS, :own]
    up_bias_ref[...] = jnp.concatenate(
        [rows[UP_BIAS + p : UP_BIAS + p + 1, :own] for p in range(up_bias_ref.shape[1] // own)], axis=1
    )
    for ref, r in zip(vector_refs, (CONV_BIAS, GAIN, SHIFT, DOWN_BIAS, SCALE)):
        ref[...] = rows[r : r + 1, :own]


def on_device(chips, first_input, second_input, cotangent, lengths, *weights):
    clips, frames, width = second_input.shape
    hidden = weights[6].shape[0] * chips * 2
    tokens = clips * frames
    block = math.gcd(clips, BLOCK)
    steps = clips // block
    rows = block * frames
    core = lax.axis_index("core").astype(jnp.int32)
    matmul = 2 * tokens * width * hidden

    blocks, owners, base = gather_weights(weights, chips * 2)

    clip_spec = pl.BlockSpec((block, frames, width), lambda i: (i, 0, 0))
    half = math.gcd(clips, BLOCK // 2)
    half_clip = pl.BlockSpec((half, frames, width), lambda i: (i, 0, 0))
    last = clips // half - 1
    later_clip = pl.BlockSpec((half, frames, width), lambda i: (jnp.minimum(i + 1, last), 0, 0))
    half_pad = pltpu.VMEM((half, width // LANES, frames + 2 * HALO, LANES), f32)
    half_row = lambda n: pl.BlockSpec((half * frames, n), lambda i: (i, 0))
    clip_out = (shape(second_input.shape, bf16), clip_spec)
    pad = pltpu.VMEM((block, width // LANES, frames + 2 * HALO, LANES), f32)

    second_output, xhat, slope, rstd, up, down, small, bias, gdown, down_grad_rows = kernel_call(
        functools.partial(second_forward, owners),
        "second_forward",
        (lengths, base, second_input, second_input, cotangent, *blocks),
        [smem(), smem(), half_clip, later_clip, half_clip] + [whole(b.shape) for b in blocks],
        [
            (shape(second_input.shape, bf16), half_clip),
            (shape((tokens, width), bf16), half_row(width)),
            (shape((tokens, hidden), bf16), half_row(hidden)),
            (shape((tokens, LANES), f32), half_row(LANES)),
            (shape((width, hidden), bf16), whole((width, hidden))),
            (shape((hidden, width), bf16), whole((hidden, width))),
            (shape((SMALL, width), f32), whole((SMALL, width))),
            (shape((8, hidden), f32), whole((8, hidden))),
            (shape((hidden, width), bf16), whole((hidden, width))),
            (shape((8, width), f32), whole((8, width))),
        ],
        [
            half_pad,
            pltpu.VMEM((half * frames, hidden), bf16),
            pltpu.VMEM((half * frames, width), bf16),
            pltpu.VMEM((width, hidden), f32),
            pltpu.VMEM((8, width), f32),
            pltpu.VMEM((half * frames, width), bf16),
            pltpu.VMEM((half * frames, LANES), f32),
        ],
        clips // half,
        3 * matmul,
        2 * tokens * hidden,
    )

    devices = chips * 2
    fast = quick(width, hidden, devices)
    if fast:
        gdown_parts = lax.all_to_all(gdown.reshape(devices, hidden // devices, width), AXES, 0, 0, tiled=True)
        payload = shape((chips, hidden // LANES * 16 + SMALL, LANES), bf16)
        outs = [(payload, whole(payload.shape))] * 2
    else:
        outs = [
            (shape((width, hidden), bf16), whole((width, hidden))),
            (shape((SMALL, width), f32), whole((SMALL, width))),
        ]

    input_grad, out_a, out_b = kernel_call(
        functools.partial(second_backward, fast),
        "second_backward",
        (lengths, core.reshape(1), cotangent, second_input, xhat, slope, rstd, up, down, small, down_grad_rows, gdown),
        [
            smem(), smem(), half_clip, half_clip, half_row(width), half_row(hidden), half_row(LANES),
            whole(up.shape), whole(down.shape), whole(small.shape), whole(down_grad_rows.shape),
            pl.BlockSpec(memory_space=pl.ANY),
        ],
        [
            (shape(second_input.shape, bf16), half_clip),
            *outs,
        ],
        [
            half_pad,
            pltpu.VMEM((half * frames, hidden), bf16),
            pltpu.VMEM((half * frames, width), bf16),
            pltpu.VMEM((width, hidden), f32),
            pltpu.VMEM((8, hidden), f32),
            pltpu.VMEM((TAPS + 1, 8, width), f32),
        ],
        clips // half,
        3 * matmul,
        0,
    )

    if fast:
        got = flipped(out_b, 1, devices)
        got, gdown_parts = lax.optimization_barrier((got, gdown_parts))
        flat = (-1, LANES)
        gup_pair = (out_a.reshape(flat).astype(f32) + got.reshape(flat).astype(f32)).astype(bf16).reshape(out_a.shape)
        gup_parts = lax.all_to_all(gup_pair, CHIPS, 0, 0, tiled=True)
    else:
        gup_pair, gdown_parts = out_a, gdown[None]

    down_shape = gdown_parts.shape
    columns = width // steps if width % (steps * LANES) == 0 else width
    part = lambda i: i if columns < width else 0
    first_output, grad_down = kernel_call(
        first_forward,
        "first_forward",
        (lengths, first_input, up, down, small, bias, gup_pair, gdown_parts, small),
        [
            smem(), clip_spec, whole(up.shape), whole(down.shape), whole(small.shape), whole(bias.shape),
            pl.BlockSpec(memory_space=pl.ANY),
            pl.BlockSpec(down_shape[:2] + (columns,), lambda i: (0, 0, part(i))),
            pl.BlockSpec((SMALL, columns), lambda i: (0, part(i))),
        ],
        [
            clip_out,
            (shape(down_shape[1:], f32), pl.BlockSpec((down_shape[1], columns), lambda i: (0, part(i)))),
        ],
        [pad, pltpu.VMEM((rows, width), bf16), pltpu.VMEM((rows, hidden), bf16)],
        steps,
        2 * matmul,
        tokens * hidden,
    )

    own = width // devices
    if fast:
        vector = shape((1, own), f32)
        grad_up, grad_taps, grad_up_bias, *vectors = pl.pallas_call(
            finish,
            out_shape=[shape((own, hidden), f32), shape((TAPS, own), f32), shape((1, hidden // devices), f32)] + [vector] * 5,
            name="finish",
        )(gup_parts)
        grad_up_bias = grad_up_bias.reshape(-1)
        vectors = [v.reshape(-1) for v in vectors]
    else:
        scatter = lambda a: lax.psum_scatter(a.astype(f32), AXES, scatter_dimension=0, tiled=True)
        me = lax.axis_index(AXES)
        grad_down = scatter(grad_down)
        grad_up = scatter(out_a)
        sums = lax.psum(out_b, AXES)
        vectors = [lax.dynamic_slice(sums[r], (me * own,), (own,)) for r in (CONV_BIAS, GAIN, SHIFT, DOWN_BIAS, SCALE)]
        grad_taps = lax.dynamic_slice(sums, (0, me * own), (TAPS, own))
        grad_up_bias = lax.dynamic_slice(
            sums[UP_BIAS : UP_BIAS + hidden // width].reshape(-1), (me * (hidden // devices),), (hidden // devices,)
        )
    conv_bias, gain, shift, down_bias, scale = vectors
    return (
        first_output,
        second_output,
        input_grad,
        grad_taps,
        conv_bias,
        gain,
        shift,
        grad_up,
        grad_up_bias,
        grad_down,
        down_bias,
        scale,
    )


def solution(mesh):
    wide, narrow = mesh.devices.shape
    grid = Mesh(mesh.devices.reshape(wide, narrow // 2, 2), AXES)
    chips = wide * narrow // 2
    rows = P(AXES)
    columns = P(None, AXES)

    def run(*args):
        return on_device(chips, *args)

    return jax.shard_map(
        run,
        mesh=grid,
        in_specs=(rows, rows, rows, rows, columns, rows, rows, rows, rows, rows, rows, rows, rows),
        out_specs=(rows, rows, rows, columns, rows, rows, rows, rows, rows, rows, rows, rows),
        check_vma=False,
    )
```

```python
import functools
import math

import jax
import jax.numpy as jnp
from jax import lax
from jax.experimental import pallas as pl
from jax.experimental.pallas import tpu as pltpu
from jax.sharding import Mesh
from jax.sharding import PartitionSpec as P

bf16, f32 = jnp.bfloat16, jnp.float32
AXES = ("wide", "half", "core")
CHIPS = ("wide", "half")
ROOT = math.sqrt(0.5)
LANES = 128
HALO = 8
TAIL = 32
CHUNK = 16
SMALL = 16
VMEM = 60 * 2**20
BLOCK = 4

TAPS = 7
CONV_BIAS, GAIN, SHIFT, DOWN_BIAS, SCALE, UP_BIAS = 7, 8, 9, 10, 11, 12


def dot(a, b, ca=1, cb=0, precision=None):
    return lax.dot_general(
        a, b, (((ca,), (cb,)), ((), ())), precision=precision, preferred_element_type=f32
    )


def whole(shape):
    return pl.BlockSpec(shape, lambda i: (0,) * len(shape))


def smem():
    return pl.BlockSpec(memory_space=pltpu.SMEM)


def tail_mask(frames, length, width):
    row = lax.broadcasted_iota(jnp.int32, (TAIL, width), 0) + (frames - TAIL)
    return row < length


def fill_padded(x_ref, m, length, pad_ref):
    frames = x_ref.shape[1]
    body = frames - TAIL
    keep = tail_mask(frames, length, LANES)
    for c in range(x_ref.shape[2] // LANES):
        cs = slice(c * LANES, (c + 1) * LANES)
        x = x_ref[m, :, cs].astype(f32)
        pad_ref[m, c, HALO : HALO + body] = x[:body]
        pad_ref[m, c, HALO + body : HALO + frames] = jnp.where(keep, x[body:], 0.0)


def clear_halo(pad_ref, frames):
    zeros = jnp.zeros(pad_ref.shape[:2] + (HALO, LANES), f32)
    pad_ref[:, :, :HALO] = zeros
    pad_ref[:, :, HALO + frames :] = zeros


def conv_norm(pad_ref, m, small_ref, frames):
    parts = []
    for c in range(pad_ref.shape[1]):
        cs = slice(c * LANES, (c + 1) * LANES)
        acc = small_ref[CONV_BIAS : CONV_BIAS + 1, cs]
        for k in range(TAPS):
            start = HALO + k - TAPS // 2
            acc = acc + small_ref[k : k + 1, cs] * pad_ref[m, c, start : start + frames]
        parts.append(acc)
    conv = jnp.concatenate(parts, axis=1)
    centred = conv - jnp.mean(conv, axis=-1, keepdims=True)
    rstd = lax.rsqrt(jnp.mean(centred * centred, axis=-1, keepdims=True) + 1e-06)
    normed = centred * rstd * small_ref[GAIN : GAIN + 1] + small_ref[SHIFT : SHIFT + 1]
    return normed.astype(bf16)


def conv_norm_into(pad_ref, m, small_ref, frames, xhat_ref, normed_ref, rstd_ref):
    width = xhat_ref.shape[1]
    for r in range(0, frames, CHUNK):
        parts = []
        for c in range(width // LANES):
            cs = slice(c * LANES, (c + 1) * LANES)
            acc = small_ref[CONV_BIAS : CONV_BIAS + 1, cs]
            for k in range(TAPS):
                start = HALO + k - TAPS // 2 + r
                acc = acc + small_ref[k : k + 1, cs] * pad_ref[m, c, start : start + CHUNK]
            parts.append(acc)
        mean = jnp.sum(sum(parts[1:], parts[0]), axis=-1, keepdims=True) / width
        parts = [p - mean for p in parts]
        square = sum((p * p for p in parts[1:]), parts[0] * parts[0])
        rstd = lax.rsqrt(jnp.sum(square, axis=-1, keepdims=True) / width + 1e-06)
        rows = slice(m * frames + r, m * frames + r + CHUNK)
        rstd_ref[rows] = jnp.broadcast_to(rstd, (CHUNK, LANES))
        for c, p in enumerate(parts):
            cs = slice(c * LANES, (c + 1) * LANES)
            xhat = p * rstd
            xhat_ref[rows, cs] = xhat.astype(bf16)
            normed = xhat * small_ref[GAIN : GAIN + 1, cs] + small_ref[SHIFT : SHIFT + 1, cs]
            normed_ref[rows, cs] = normed.astype(bf16)


def store_output(out_ref, m, length, x_ref, branch):
    frames = x_ref.shape[1]
    body = frames - TAIL
    keep = tail_mask(frames, length, x_ref.shape[2])
    value = x_ref[m].astype(f32) + branch
    out_ref[m, :body] = value[:body].astype(bf16)
    out_ref[m, body:] = jnp.where(keep, value[body:], 0.0).astype(bf16)


def store_masked(dst_ref, m, length, src_ref):
    frames = src_ref.shape[1]
    body = frames - TAIL
    keep = tail_mask(frames, length, src_ref.shape[2])
    at = m * frames
    dst_ref[at : at + body] = src_ref[m, :body]
    dst_ref[at + body : at + frames] = jnp.where(keep, src_ref[m, body:].astype(f32), 0.0).astype(bf16)


def second_forward(
    owners, len_ref, me_ref, x_ref, next_ref, cot_ref, *refs
):
    count = len(refs) - 18
    block_refs = [ref.at[j] for ref in refs[:count] for j in range(ref.shape[0])]
    second_forward_body(owners, len_ref, me_ref, x_ref, next_ref, cot_ref, block_refs, *refs[count:])


def second_forward_body(
    owners, len_ref, me_ref, x_ref, next_ref, cot_ref, block_refs,
    out_ref, xhat_ref, slope_ref, rstd_ref, up_ref, down_ref, small_ref, bias_ref, gdown_ref, rows_ref,
    pad_ref, act_ref, mcot_ref, acc_ref, csum_ref, xnext_ref, normed_ref, rnext_ref,
):
    step = pl.program_id(0)
    clips, frames, width = x_ref.shape
    hidden = up_ref.shape[1]
    parts = hidden // width

    @pl.when(step == 0)
    def _():
        devices = len(block_refs)
        up_rows, down_rows = width // devices, hidden // devices
        clear_halo(pad_ref, frames)
        small = jnp.zeros((SMALL, width), f32)
        for ref in block_refs:
            small = small + ref[2 * down_rows :].astype(f32)
        small_ref[...] = small
        scale = small[SCALE : SCALE + 1] * 0.5
        for j, ref in enumerate(block_refs):
            owner = me_ref[0] ^ owners[j]
            at = pl.multiple_of(owner * up_rows, up_rows)
            for p in range(parts):
                up_ref[pl.ds(at, up_rows), p * width : (p + 1) * width] = ref[p * up_rows : (p + 1) * up_rows]
            at = pl.multiple_of(owner * down_rows, down_rows)
            down_ref[pl.ds(at, down_rows)] = (ref[down_rows : 2 * down_rows].astype(f32) * scale).astype(bf16)
        for p in range(parts):
            bias = small[UP_BIAS + p : UP_BIAS + p + 1]
            bias_ref[:, p * width : (p + 1) * width] = jnp.broadcast_to(bias, (8, width))
        acc_ref[...] = jnp.zeros_like(acc_ref)
        csum_ref[...] = jnp.zeros_like(csum_ref)
        for m in range(clips):
            fill_padded(x_ref, m, len_ref[m], pad_ref)
            conv_norm_into(pad_ref, m, small_ref, frames, xnext_ref, normed_ref, rnext_ref)

    lengths = [len_ref[step * clips + m] for m in range(clips)]
    xhat_ref[...] = xnext_ref[...]
    rstd_ref[...] = rnext_ref[...]
    for m in range(clips):
        store_masked(mcot_ref, m, lengths[m], cot_ref)

    for p in range(parts):
        cs = slice(p * width, (p + 1) * width)
        u = dot(normed_ref[...], up_ref[:, cs]) + bias_ref[0:1, cs]
        s = 1.0 + lax.erf(u * ROOT)
        act_ref[:, cs] = (u * s).astype(bf16)
        bell = jnp.exp2(u * u * (-0.5 * math.log2(math.e)))
        slope_ref[:, cs] = (s + u * bell * math.sqrt(2.0 / math.pi)).astype(bf16)

    down_bias = small_ref[DOWN_BIAS : DOWN_BIAS + 1] * small_ref[SCALE : SCALE + 1]
    branch = dot(act_ref[...], down_ref[...]) + down_bias
    for m in range(clips):
        store_output(out_ref, m, lengths[m], x_ref, branch[m * frames : (m + 1) * frames])

    acc_ref[...] += dot(mcot_ref[...], act_ref[...], 0, 0)
    csum_ref[...] += jnp.sum(mcot_ref[...].astype(f32).reshape(-1, 8, width), axis=0)
    later = jnp.minimum(step + 1, pl.num_programs(0) - 1) * clips
    for m in range(clips):
        fill_padded(next_ref, m, len_ref[later + m], pad_ref)
        conv_norm_into(pad_ref, m, small_ref, frames, xnext_ref, normed_ref, rnext_ref)

    @pl.when(step == pl.num_programs(0) - 1)
    def _():
        total = acc_ref[...].T
        gdown_ref[...] = total.astype(bf16)
        scale = small_ref[SCALE : SCALE + 1]
        csum = jnp.sum(csum_ref[...], axis=0, keepdims=True)
        cross = jnp.sum(total * down_ref[...].astype(f32), axis=0, keepdims=True)
        rows_ref[0:1] = csum * scale
        rows_ref[1:2] = cross / scale + csum * small_ref[DOWN_BIAS : DOWN_BIAS + 1]
        rows_ref[2:8] = jnp.zeros((6, width), f32)


def second_backward(
    packed, len_ref, core_ref, cot_ref, x_ref, xhat_ref, slope_ref, rstd_ref, up_ref, down_ref, small_ref, down_rows_ref, _,
    grad_ref, out_a_ref, out_b_ref,
    pad_ref, gh_ref, mcot_ref, acc_ref, hsum_ref, tsum_ref,
):
    step = pl.program_id(0)
    clips, frames, width = x_ref.shape
    hidden = up_ref.shape[1]
    parts = hidden // width

    @pl.when(step == 0)
    def _():
        clear_halo(pad_ref, frames)
        acc_ref[...] = jnp.zeros_like(acc_ref)
        hsum_ref[...] = jnp.zeros_like(hsum_ref)
        tsum_ref[...] = jnp.zeros_like(tsum_ref)

    lengths = [len_ref[step * clips + m] for m in range(clips)]
    for m in range(clips):
        store_masked(mcot_ref, m, lengths[m], cot_ref)
    for m in range(clips):
        rows = slice(m * frames, (m + 1) * frames)
        for p in range(parts):
            cs = slice(p * width, (p + 1) * width)
            ga = dot(mcot_ref[rows], down_ref[cs, :], 1, 1)
            gh = ga * slope_ref[rows, cs].astype(f32)
            hsum_ref[:, cs] += jnp.sum(gh.reshape(-1, 8, width), axis=0)
            gh_ref[rows, cs] = gh.astype(bf16)
    for m in range(clips):
        rows = slice(m * frames, (m + 1) * frames)
        g = dot(gh_ref[rows], up_ref[...], 1, 1) * small_ref[GAIN : GAIN + 1]
        xhat = xhat_ref[rows].astype(f32)
        mean = jnp.mean(g, axis=-1, keepdims=True)
        proj = jnp.mean(g * xhat, axis=-1, keepdims=True)
        rstd = rstd_ref[rows]
        for c in range(width // LANES):
            cs = slice(c * LANES, (c + 1) * LANES)
            gc = (g[:, cs] - mean - xhat[:, cs] * proj) * rstd
            pad_ref[m, c, HALO : HALO + frames] = gc
            tsum_ref[TAPS, :, cs] += jnp.sum(gc.reshape(-1, 8, LANES), axis=0)
    acc_ref[...] += dot(xhat_ref[...], gh_ref[...], 0, 0)
    for m in range(clips):
        keep = tail_mask(frames, lengths[m], LANES)
        for c in range(width // LANES):
            cs = slice(c * LANES, (c + 1) * LANES)
            sums = [jnp.zeros((8, LANES), f32)] * TAPS
            for r in range(0, frames, TAIL):
                x = x_ref[m, r : r + TAIL, cs].astype(f32)
                total = cot_ref[m, r : r + TAIL, cs].astype(f32)
                if r + TAIL == frames:
                    x = jnp.where(keep, x, 0.0)
                for k in range(TAPS):
                    start = HALO + TAPS // 2 - k + r
                    gc = pad_ref[m, c, start : start + TAIL]
                    total = total + small_ref[k : k + 1, cs] * gc
                    sums[k] = sums[k] + jnp.sum((gc * x).reshape(-1, 8, LANES), axis=0)
                if r + TAIL == frames:
                    total = jnp.where(keep, total, 0.0)
                grad_ref[m, r : r + TAIL, cs] = total.astype(bf16)
            for k in range(TAPS):
                tsum_ref[k, :, cs] += sums[k]

    @pl.when(step == pl.num_programs(0) - 1)
    def _():
        total = acc_ref[...]
        hsum = jnp.sum(hsum_ref[...], axis=0, keepdims=True)
        columns = small_ref[...].T
        gain, shift = columns[:, GAIN : GAIN + 1], columns[:, SHIFT : SHIFT + 1]
        rows = [jnp.sum(tsum_ref[k], axis=0, keepdims=True) for k in range(TAPS + 1)]
        up = up_ref[...].astype(f32)
        for value in (up * total, up * hsum):
            part = value[:, :LANES]
            for c in range(1, hidden // LANES):
                part = part + value[:, c * LANES : (c + 1) * LANES]
            rows.append(jnp.sum(part.T, axis=0, keepdims=True))
        rows.append(down_rows_ref[0:2])
        if not packed:
            out_a_ref[...] = (gain * total + shift * hsum).astype(bf16)
            rows += [hsum[:, p * width : (p + 1) * width] for p in range(parts)]
            rows.append(jnp.zeros((SMALL - UP_BIAS - parts, width), f32))
            out_b_ref[...] = jnp.concatenate(rows, axis=0)
            return
        rows.append(jnp.zeros((SMALL - UP_BIAS, width), f32))
        rows = jnp.concatenate(rows, axis=0)
        bias = hsum
        lane = lax.broadcasted_iota(jnp.int32, (SMALL, LANES), 1)
        line = lax.broadcasted_iota(jnp.int32, (SMALL, LANES), 0)
        devices = width // 16
        even = core_ref[0] == 0
        acc_ref[...] = gain * total + shift * hsum
        for chip in range(devices // 2):
            for ref, core in ((out_a_ref, core_ref[0]), (out_b_ref, 1 - core_ref[0])):
                at = pl.multiple_of(chip * 32 + core * 16, 16)
                for c in range(hidden // LANES):
                    value = acc_ref[pl.ds(at, 16), c * LANES : (c + 1) * LANES]
                    ref[chip, c * 16 : (c + 1) * 16] = value.astype(bf16)
        pair = []
        for owner in range(devices):
            at = owner * 16 // LANES * LANES
            mine = pltpu.roll(rows[:, at : at + LANES], (LANES - owner * 16 % LANES) % LANES, 1)
            for r in range(parts):
                first = owner * 16 * parts + r * 16
                at = first // LANES * LANES
                part = pltpu.roll(
                    jnp.broadcast_to(bias[:, at : at + LANES], (SMALL, LANES)), (LANES - first % LANES) % LANES, 1
                )
                mine = jnp.where(line == UP_BIAS + r, part, mine)
            high = mine.astype(bf16).astype(f32)
            low = pltpu.roll(mine - high, LANES // 2, 1)
            pair.append(jnp.where(lane < 16, high, jnp.where((lane >= LANES // 2) & (lane < LANES // 2 + 16), low, 0.0)))
            if owner % 2:
                first, second = pair[-2:]
                out_a_ref[owner // 2, hidden // LANES * 16 :] = jnp.where(even, first, second).astype(bf16)
                out_b_ref[owner // 2, hidden // LANES * 16 :] = jnp.where(even, second, first).astype(bf16)


def first_forward(
    len_ref, x_ref, up_ref, down_ref, small_ref, bias_ref, _, parts_ref, scale_ref,
    out_ref, grad_down_ref,
    pad_ref, xhat_ref, act_ref,
):
    total = jnp.zeros(parts_ref.shape[1:], f32)
    for j in range(parts_ref.shape[0]):
        total = total + parts_ref[j].astype(f32)
    grad_down_ref[...] = total * (scale_ref[SCALE : SCALE + 1] * 0.5)

    step = pl.program_id(0)
    clips, frames, width = x_ref.shape
    parts = up_ref.shape[1] // width

    @pl.when(step == 0)
    def _():
        clear_halo(pad_ref, frames)

    lengths = [len_ref[step * clips + m] for m in range(clips)]
    down_bias = small_ref[DOWN_BIAS : DOWN_BIAS + 1] * small_ref[SCALE : SCALE + 1]

    def front(m):
        fill_padded(x_ref, m, lengths[m], pad_ref)
        xhat_ref[m * frames : (m + 1) * frames] = conv_norm(pad_ref, m, small_ref, frames)

    front(0)
    for m in range(clips):
        if m + 1 < clips:
            front(m + 1)
        rows = slice(m * frames, (m + 1) * frames)
        for p in range(2 * parts):
            cs = slice(p * width // 2, (p + 1) * width // 2)
            u = dot(xhat_ref[rows], up_ref[:, cs]) + bias_ref[0:1, cs]
            act_ref[rows, cs] = (u * (1.0 + lax.erf(u * ROOT))).astype(bf16)
        store_output(out_ref, m, lengths[m], x_ref, dot(act_ref[rows], down_ref[...]) + down_bias)


def kernel_call(body, name, args, specs, outs, scratch, steps, flops, elements):
    def size(a):
        return math.prod(a.shape) * jnp.dtype(a.dtype).itemsize

    return pl.pallas_call(
        body,
        grid=(steps,),
        in_specs=specs,
        out_specs=[spec for _, spec in outs],
        out_shape=[shape for shape, _ in outs],
        scratch_shapes=scratch,
        compiler_params=pltpu.CompilerParams(vmem_limit_bytes=VMEM),
        cost_estimate=pl.CostEstimate(
            flops=flops,
            bytes_accessed=sum(map(size, args)) + sum(size(s) for s, _ in outs),
            transcendentals=elements,
        ),
        name=name,
    )(*args)


def shape(dims, dtype):
    return jax.ShapeDtypeStruct(dims, dtype)


def own_block(
    me_ref, conv_ref, conv_bias_ref, gain_ref, shift_ref, up_ref, up_bias_ref, down_ref, down_bias_ref, scale_ref,
    block_ref,
    row_ref,
):
    own, hidden = up_ref.shape
    rows, width = down_ref.shape
    parts = hidden // width
    me = me_ref[0]
    for p in range(parts):
        block_ref[p * own : (p + 1) * own] = up_ref[:, p * width : (p + 1) * width]
    block_ref[rows : 2 * rows] = down_ref[...]
    vectors = [r[...].astype(f32) for r in (conv_bias_ref, gain_ref, shift_ref, down_bias_ref, scale_ref)]
    small = jnp.concatenate([conv_ref[...].astype(f32)] + vectors + [jnp.zeros((SMALL - UP_BIAS, own), f32)], axis=0)
    small = jnp.concatenate([small, jnp.zeros((SMALL, LANES - own), f32)], axis=1)
    row_ref[...] = jnp.zeros_like(row_ref)
    per = LANES // own
    at = pl.multiple_of(me // per * LANES, LANES)
    row_ref[:, pl.ds(at, LANES)] = pltpu.roll(small, me % per * own, 1)
    bias = jnp.concatenate([up_bias_ref[...].astype(f32), jnp.zeros((1, 2 * LANES - rows), f32)], axis=1)
    bias = pltpu.roll(jnp.broadcast_to(bias, (8, 2 * LANES)), me * rows % LANES, 1)
    first = me * rows // LANES
    tiles = width // LANES
    for t in range(hidden // LANES):
        part = jnp.where(first == t, bias[:1, :LANES], jnp.where(first + 1 == t, bias[:1, LANES:], 0.0))
        row_ref[UP_BIAS + t // tiles : UP_BIAS + t // tiles + 1, t % tiles * LANES : (t % tiles + 1) * LANES] = part

    block_ref[2 * rows :] = row_ref[...].astype(bf16)


def quick(width, hidden, devices):
    return devices == 32 and width == 16 * devices and hidden % width == 0


def flipped(a, bits, devices):
    return lax.ppermute(a, AXES, [(i, i ^ bits) for i in range(devices)])


def gather_weights(weights, devices):
    conv_weight, conv_bias, gain, shift, up, up_bias, down, down_bias, scale = weights
    up_rows, hidden = up.shape
    down_rows, width = down.shape
    parts = hidden // width
    me = lax.axis_index(AXES).astype(jnp.int32)
    if quick(width, hidden, devices):
        row = lambda v: v.reshape(1, -1)
        args = (me.reshape(1), conv_weight, row(conv_bias), row(gain), row(shift), up, row(up_bias), down, row(down_bias), row(scale))
        block = pl.pallas_call(
            own_block,
            in_specs=[smem()] + [pl.BlockSpec(memory_space=pltpu.VMEM)] * 9,
            out_specs=pl.BlockSpec(memory_space=pltpu.VMEM),
            out_shape=shape((2 * down_rows + SMALL, width), bf16),
            scratch_shapes=[pltpu.VMEM((SMALL, width), f32)],
            name="own_block",
        )(*args)
        both = jnp.stack([block, flipped(block, 16, devices)])
        have = {0: both}
        for flip, start in ((8, 0), (4, 0), (2, 0), (2, 4), (8, 2), (4, 8), (8, 6)):
            have[flip ^ start] = flipped(have[start], flip, devices)
        for start in list(have):
            have[start ^ 1] = flipped(have[start], 1, devices)
        order = [start ^ far for start in have for far in (0, 16)]
        return list(have.values()), order, me.reshape(1)
    everyone = lambda a, axis: lax.all_gather(a, AXES, axis=axis, tiled=True)
    up, down, up_bias = everyone(up, 0), everyone(down, 0), everyone(up_bias, 0)
    vectors = jnp.stack([conv_bias, gain, shift, down_bias, scale])
    small = jnp.concatenate([everyone(conv_weight, 1), everyone(vectors, 1), up_bias.reshape(parts, width)], axis=0)
    small = jnp.pad(small, ((0, SMALL - small.shape[0]), (0, 0)))
    count = width // 16
    up = up.reshape(count, 16, parts, width).swapaxes(1, 2).reshape(count, 16 * parts, width)
    down = down.reshape(count, 16 * parts, width)
    small = jnp.pad(small[None], ((0, count - 1), (0, 0), (0, 0)))
    return [jnp.concatenate([up, down, small], axis=1)], list(range(count)), jnp.zeros((1,), jnp.int32)


def finish(parts_ref, grad_up_ref, taps_ref, up_bias_ref, *vector_refs):
    total = jnp.zeros(parts_ref.shape[1:], f32)
    for j in range(parts_ref.shape[0]):
        total = total + parts_ref[j].astype(f32)
    own, hidden = grad_up_ref.shape
    for c in range(hidden // LANES):
        grad_up_ref[:, c * LANES : (c + 1) * LANES] = total[c * own : (c + 1) * own]
    rows = total[hidden // LANES * own :]
    rows = rows + pltpu.roll(rows, LANES // 2, 1)
    taps_ref[...] = rows[:TAPS, :own]
    up_bias_ref[...] = jnp.concatenate(
        [rows[UP_BIAS + p : UP_BIAS + p + 1, :own] for p in range(up_bias_ref.shape[1] // own)], axis=1
    )
    for ref, r in zip(vector_refs, (CONV_BIAS, GAIN, SHIFT, DOWN_BIAS, SCALE)):
        ref[...] = rows[r : r + 1, :own]


def on_device(chips, first_input, second_input, cotangent, lengths, *weights):
    clips, frames, width = second_input.shape
    hidden = weights[6].shape[0] * chips * 2
    tokens = clips * frames
    block = math.gcd(clips, BLOCK)
    steps = clips // block
    rows = block * frames
    core = lax.axis_index("core").astype(jnp.int32)
    matmul = 2 * tokens * width * hidden

    blocks, owners, base = gather_weights(weights, chips * 2)

    clip_spec = pl.BlockSpec((block, frames, width), lambda i: (i, 0, 0))
    half = math.gcd(clips, BLOCK // 2)
    half_clip = pl.BlockSpec((half, frames, width), lambda i: (i, 0, 0))
    last = clips // half - 1
    later_clip = pl.BlockSpec((half, frames, width), lambda i: (jnp.minimum(i + 1, last), 0, 0))
    half_pad = pltpu.VMEM((half, width // LANES, frames + 2 * HALO, LANES), f32)
    half_row = lambda n: pl.BlockSpec((half * frames, n), lambda i: (i, 0))
    clip_out = (shape(second_input.shape, bf16), clip_spec)
    pad = pltpu.VMEM((block, width // LANES, frames + 2 * HALO, LANES), f32)

    second_output, xhat, slope, rstd, up, down, small, bias, gdown, down_grad_rows = kernel_call(
        functools.partial(second_forward, owners),
        "second_forward",
        (lengths, base, second_input, second_input, cotangent, *blocks),
        [smem(), smem(), half_clip, later_clip, half_clip] + [whole(b.shape) for b in blocks],
        [
            (shape(second_input.shape, bf16), half_clip),
            (shape((tokens, width), bf16), half_row(width)),
            (shape((tokens, hidden), bf16), half_row(hidden)),
            (shape((tokens, LANES), f32), half_row(LANES)),
            (shape((width, hidden), bf16), whole((width, hidden))),
            (shape((hidden, width), bf16), whole((hidden, width))),
            (shape((SMALL, width), f32), whole((SMALL, width))),
            (shape((8, hidden), f32), whole((8, hidden))),
            (shape((hidden, width), bf16), whole((hidden, width))),
            (shape((8, width), f32), whole((8, width))),
        ],
        [
            half_pad,
            pltpu.VMEM((half * frames, hidden), bf16),
            pltpu.VMEM((half * frames, width), bf16),
            pltpu.VMEM((width, hidden), f32),
            pltpu.VMEM((8, width), f32),
            pltpu.VMEM((half * frames, width), bf16),
            pltpu.VMEM((half * frames, width), bf16),
            pltpu.VMEM((half * frames, LANES), f32),
        ],
        clips // half,
        3 * matmul,
        2 * tokens * hidden,
    )

    devices = chips * 2
    fast = quick(width, hidden, devices)
    if fast:
        gdown_parts = lax.all_to_all(gdown.reshape(devices, hidden // devices, width), AXES, 0, 0, tiled=True)
        payload = shape((chips, hidden // LANES * 16 + SMALL, LANES), bf16)
        outs = [(payload, whole(payload.shape))] * 2
    else:
        outs = [
            (shape((width, hidden), bf16), whole((width, hidden))),
            (shape((SMALL, width), f32), whole((SMALL, width))),
        ]

    input_grad, out_a, out_b = kernel_call(
        functools.partial(second_backward, fast),
        "second_backward",
        (lengths, core.reshape(1), cotangent, second_input, xhat, slope, rstd, up, down, small, down_grad_rows, gdown),
        [
            smem(), smem(), half_clip, half_clip, half_row(width), half_row(hidden), half_row(LANES),
            whole(up.shape), whole(down.shape), whole(small.shape), whole(down_grad_rows.shape),
            pl.BlockSpec(memory_space=pl.ANY),
        ],
        [
            (shape(second_input.shape, bf16), half_clip),
            *outs,
        ],
        [
            half_pad,
            pltpu.VMEM((half * frames, hidden), bf16),
            pltpu.VMEM((half * frames, width), bf16),
            pltpu.VMEM((width, hidden), f32),
            pltpu.VMEM((8, hidden), f32),
            pltpu.VMEM((TAPS + 1, 8, width), f32),
        ],
        clips // half,
        3 * matmul,
        0,
    )

    if fast:
        got = flipped(out_b, 1, devices)
        got, gdown_parts = lax.optimization_barrier((got, gdown_parts))
        flat = (-1, LANES)
        gup_pair = (out_a.reshape(flat).astype(f32) + got.reshape(flat).astype(f32)).astype(bf16).reshape(out_a.shape)
        gup_parts = lax.all_to_all(gup_pair, CHIPS, 0, 0, tiled=True)
    else:
        gup_pair, gdown_parts = out_a, gdown[None]

    down_shape = gdown_parts.shape
    columns = width // steps if width % (steps * LANES) == 0 else width
    part = lambda i: i if columns < width else 0
    first_output, grad_down = kernel_call(
        first_forward,
        "first_forward",
        (lengths, first_input, up, down, small, bias, gup_pair, gdown_parts, small),
        [
            smem(), clip_spec, whole(up.shape), whole(down.shape), whole(small.shape), whole(bias.shape),
            pl.BlockSpec(memory_space=pl.ANY),
            pl.BlockSpec(down_shape[:2] + (columns,), lambda i: (0, 0, part(i))),
            pl.BlockSpec((SMALL, columns), lambda i: (0, part(i))),
        ],
        [
            clip_out,
            (shape(down_shape[1:], f32), pl.BlockSpec((down_shape[1], columns), lambda i: (0, part(i)))),
        ],
        [pad, pltpu.VMEM((rows, width), bf16), pltpu.VMEM((rows, hidden), bf16)],
        steps,
        2 * matmul,
        tokens * hidden,
    )

    own = width // devices
    if fast:
        vector = shape((1, own), f32)
        grad_up, grad_taps, grad_up_bias, *vectors = pl.pallas_call(
            finish,
            out_shape=[shape((own, hidden), f32), shape((TAPS, own), f32), shape((1, hidden // devices), f32)] + [vector] * 5,
            name="finish",
        )(gup_parts)
        grad_up_bias = grad_up_bias.reshape(-1)
        vectors = [v.reshape(-1) for v in vectors]
    else:
        scatter = lambda a: lax.psum_scatter(a.astype(f32), AXES, scatter_dimension=0, tiled=True)
        me = lax.axis_index(AXES)
        grad_down = scatter(grad_down)
        grad_up = scatter(out_a)
        sums = lax.psum(out_b, AXES)
        vectors = [lax.dynamic_slice(sums[r], (me * own,), (own,)) for r in (CONV_BIAS, GAIN, SHIFT, DOWN_BIAS, SCALE)]
        grad_taps = lax.dynamic_slice(sums, (0, me * own), (TAPS, own))
        grad_up_bias = lax.dynamic_slice(
            sums[UP_BIAS : UP_BIAS + hidden // width].reshape(-1), (me * (hidden // devices),), (hidden // devices,)
        )
    conv_bias, gain, shift, down_bias, scale = vectors
    return (
        first_output,
        second_output,
        input_grad,
        grad_taps,
        conv_bias,
        gain,
        shift,
        grad_up,
        grad_up_bias,
        grad_down,
        down_bias,
        scale,
    )


def solution(mesh):
    wide, narrow = mesh.devices.shape
    grid = Mesh(mesh.devices.reshape(wide, narrow // 2, 2), AXES)
    chips = wide * narrow // 2
    rows = P(AXES)
    columns = P(None, AXES)

    def run(*args):
        return on_device(chips, *args)

    return jax.shard_map(
        run,
        mesh=grid,
        in_specs=(rows, rows, rows, rows, columns, rows, rows, rows, rows, rows, rows, rows, rows),
        out_specs=(rows, rows, rows, columns, rows, rows, rows, rows, rows, rows, rows, rows),
        check_vma=False,
    )
```

```python
import functools
import math

import jax
import jax.numpy as jnp
from jax import lax
from jax.experimental import pallas as pl
from jax.experimental.pallas import tpu as pltpu
from jax.sharding import Mesh
from jax.sharding import PartitionSpec as P

bf16, f32 = jnp.bfloat16, jnp.float32
AXES = ("wide", "half", "core")
CHIPS = ("wide", "half")
ROOT = math.sqrt(0.5)
LANES = 128
HALO = 8
TAIL = 32
CHUNK = 16
SMALL = 16
VMEM = 60 * 2**20
BLOCK = 4

TAPS = 7
CONV_BIAS, GAIN, SHIFT, DOWN_BIAS, SCALE, UP_BIAS = 7, 8, 9, 10, 11, 12


def dot(a, b, ca=1, cb=0, precision=None):
    return lax.dot_general(
        a, b, (((ca,), (cb,)), ((), ())), precision=precision, preferred_element_type=f32
    )


def whole(shape):
    return pl.BlockSpec(shape, lambda i: (0,) * len(shape))


def smem():
    return pl.BlockSpec(memory_space=pltpu.SMEM)


def tail_mask(frames, length, width):
    row = lax.broadcasted_iota(jnp.int32, (TAIL, width), 0) + (frames - TAIL)
    return row < length


def fill_padded(x_ref, m, length, pad_ref):
    frames = x_ref.shape[1]
    body = frames - TAIL
    keep = tail_mask(frames, length, LANES)
    for c in range(x_ref.shape[2] // LANES):
        cs = slice(c * LANES, (c + 1) * LANES)
        x = x_ref[m, :, cs].astype(f32)
        pad_ref[m, c, HALO : HALO + body] = x[:body]
        pad_ref[m, c, HALO + body : HALO + frames] = jnp.where(keep, x[body:], 0.0)


def clear_halo(pad_ref, frames):
    zeros = jnp.zeros(pad_ref.shape[:2] + (HALO, LANES), f32)
    pad_ref[:, :, :HALO] = zeros
    pad_ref[:, :, HALO + frames :] = zeros


def conv_norm(pad_ref, m, small_ref, frames):
    parts = []
    for c in range(pad_ref.shape[1]):
        cs = slice(c * LANES, (c + 1) * LANES)
        acc = small_ref[CONV_BIAS : CONV_BIAS + 1, cs]
        for k in range(TAPS):
            start = HALO + k - TAPS // 2
            acc = acc + small_ref[k : k + 1, cs] * pad_ref[m, c, start : start + frames]
        parts.append(acc)
    conv = jnp.concatenate(parts, axis=1)
    centred = conv - jnp.mean(conv, axis=-1, keepdims=True)
    rstd = lax.rsqrt(jnp.mean(centred * centred, axis=-1, keepdims=True) + 1e-06)
    normed = centred * rstd * small_ref[GAIN : GAIN + 1] + small_ref[SHIFT : SHIFT + 1]
    return normed.astype(bf16)


def conv_norm_into(pad_ref, m, small_ref, frames, xhat_ref, normed_ref, rstd_ref):
    width = xhat_ref.shape[1]
    for r in range(0, frames, CHUNK):
        parts = []
        for c in range(width // LANES):
            cs = slice(c * LANES, (c + 1) * LANES)
            acc = small_ref[CONV_BIAS : CONV_BIAS + 1, cs]
            for k in range(TAPS):
                start = HALO + k - TAPS // 2 + r
                acc = acc + small_ref[k : k + 1, cs] * pad_ref[m, c, start : start + CHUNK]
            parts.append(acc)
        mean = jnp.sum(sum(parts[1:], parts[0]), axis=-1, keepdims=True) / width
        parts = [p - mean for p in parts]
        square = sum((p * p for p in parts[1:]), parts[0] * parts[0])
        rstd = lax.rsqrt(jnp.sum(square, axis=-1, keepdims=True) / width + 1e-06)
        rows = slice(m * frames + r, m * frames + r + CHUNK)
        rstd_ref[rows] = jnp.broadcast_to(rstd, (CHUNK, LANES))
        for c, p in enumerate(parts):
            cs = slice(c * LANES, (c + 1) * LANES)
            xhat = p * rstd
            xhat_ref[rows, cs] = xhat.astype(bf16)
            normed = xhat * small_ref[GAIN : GAIN + 1, cs] + small_ref[SHIFT : SHIFT + 1, cs]
            normed_ref[rows, cs] = normed.astype(bf16)


def store_output(out_ref, m, length, x_ref, branch):
    frames = x_ref.shape[1]
    body = frames - TAIL
    keep = tail_mask(frames, length, x_ref.shape[2])
    value = x_ref[m].astype(f32) + branch
    out_ref[m, :body] = value[:body].astype(bf16)
    out_ref[m, body:] = jnp.where(keep, value[body:], 0.0).astype(bf16)


def store_masked(dst_ref, m, length, src_ref):
    frames = src_ref.shape[1]
    body = frames - TAIL
    keep = tail_mask(frames, length, src_ref.shape[2])
    at = m * frames
    dst_ref[at : at + body] = src_ref[m, :body]
    dst_ref[at + body : at + frames] = jnp.where(keep, src_ref[m, body:].astype(f32), 0.0).astype(bf16)


def second_forward(
    owners, len_ref, me_ref, x_ref, next_ref, cot_ref, *refs
):
    count = len(refs) - 18
    block_refs = [ref.at[j] for ref in refs[:count] for j in range(ref.shape[0])]
    second_forward_body(owners, len_ref, me_ref, x_ref, next_ref, cot_ref, block_refs, *refs[count:])


def second_forward_body(
    owners, len_ref, me_ref, x_ref, next_ref, cot_ref, block_refs,
    out_ref, xhat_ref, slope_ref, rstd_ref, up_ref, down_ref, small_ref, bias_ref, gdown_ref, rows_ref,
    pad_ref, act_ref, mcot_ref, acc_ref, csum_ref, xnext_ref, normed_ref, rnext_ref,
):
    step = pl.program_id(0)
    clips, frames, width = x_ref.shape
    hidden = up_ref.shape[1]
    parts = hidden // width

    @pl.when(step == 0)
    def _():
        devices = len(block_refs)
        up_rows, down_rows = width // devices, hidden // devices
        clear_halo(pad_ref, frames)
        small = jnp.zeros((SMALL, width), f32)
        for ref in block_refs:
            small = small + ref[2 * down_rows :].astype(f32)
        small_ref[...] = small
        scale = small[SCALE : SCALE + 1] * 0.5
        for j, ref in enumerate(block_refs):
            owner = me_ref[0] ^ owners[j]
            at = pl.multiple_of(owner * up_rows, up_rows)
            for p in range(parts):
                up_ref[pl.ds(at, up_rows), p * width : (p + 1) * width] = ref[p * up_rows : (p + 1) * up_rows]
            at = pl.multiple_of(owner * down_rows, down_rows)
            down_ref[pl.ds(at, down_rows)] = (ref[down_rows : 2 * down_rows].astype(f32) * scale).astype(bf16)
        for p in range(parts):
            bias = small[UP_BIAS + p : UP_BIAS + p + 1]
            bias_ref[:, p * width : (p + 1) * width] = jnp.broadcast_to(bias, (8, width))
        acc_ref[...] = jnp.zeros_like(acc_ref)
        csum_ref[...] = jnp.zeros_like(csum_ref)
        for m in range(clips):
            fill_padded(x_ref, m, len_ref[m], pad_ref)
            conv_norm_into(pad_ref, m, small_ref, frames, xnext_ref, normed_ref, rnext_ref)

    lengths = [len_ref[step * clips + m] for m in range(clips)]
    xhat_ref[...] = xnext_ref[...]
    rstd_ref[...] = rnext_ref[...]
    for m in range(clips):
        store_masked(mcot_ref, m, lengths[m], cot_ref)

    for p in range(parts):
        cs = slice(p * width, (p + 1) * width)
        u = dot(normed_ref[...], up_ref[:, cs]) + bias_ref[0:1, cs]
        s = 1.0 + lax.erf(u * ROOT)
        act_ref[:, cs] = (u * s).astype(bf16)
        bell = jnp.exp2(u * u * (-0.5 * math.log2(math.e)))
        slope_ref[:, cs] = (s + u * bell * math.sqrt(2.0 / math.pi)).astype(bf16)

    down_bias = small_ref[DOWN_BIAS : DOWN_BIAS + 1] * small_ref[SCALE : SCALE + 1]
    branch = dot(act_ref[...], down_ref[...]) + down_bias
    for m in range(clips):
        store_output(out_ref, m, lengths[m], x_ref, branch[m * frames : (m + 1) * frames])

    acc_ref[...] += dot(mcot_ref[...], act_ref[...], 0, 0)
    csum_ref[...] += jnp.sum(mcot_ref[...].astype(f32).reshape(-1, 8, width), axis=0)
    later = jnp.minimum(step + 1, pl.num_programs(0) - 1) * clips
    for m in range(clips):
        fill_padded(next_ref, m, len_ref[later + m], pad_ref)
        conv_norm_into(pad_ref, m, small_ref, frames, xnext_ref, normed_ref, rnext_ref)

    @pl.when(step == pl.num_programs(0) - 1)
    def _():
        total = acc_ref[...].T
        gdown_ref[...] = total.astype(bf16)
        scale = small_ref[SCALE : SCALE + 1]
        csum = jnp.sum(csum_ref[...], axis=0, keepdims=True)
        cross = jnp.sum(total * down_ref[...].astype(f32), axis=0, keepdims=True)
        rows_ref[0:1] = csum * scale
        rows_ref[1:2] = cross / scale + csum * small_ref[DOWN_BIAS : DOWN_BIAS + 1]
        rows_ref[2:8] = jnp.zeros((6, width), f32)


def second_backward(
    packed, len_ref, core_ref, cot_ref, x_ref, xhat_ref, slope_ref, rstd_ref, up_ref, down_ref, small_ref, down_rows_ref, _,
    grad_ref, out_a_ref, out_b_ref,
    pad_ref, gh_ref, mcot_ref, acc_ref, hsum_ref, tsum_ref,
):
    step = pl.program_id(0)
    clips, frames, width = x_ref.shape
    hidden = up_ref.shape[1]
    parts = hidden // width

    @pl.when(step == 0)
    def _():
        clear_halo(pad_ref, frames)
        acc_ref[...] = jnp.zeros_like(acc_ref)
        hsum_ref[...] = jnp.zeros_like(hsum_ref)
        tsum_ref[...] = jnp.zeros_like(tsum_ref)

    lengths = [len_ref[step * clips + m] for m in range(clips)]
    for m in range(clips):
        store_masked(mcot_ref, m, lengths[m], cot_ref)
    for m in range(clips):
        rows = slice(m * frames, (m + 1) * frames)
        for p in range(parts):
            cs = slice(p * width, (p + 1) * width)
            ga = dot(mcot_ref[rows], down_ref[cs, :], 1, 1)
            gh = ga * slope_ref[rows, cs].astype(f32)
            hsum_ref[:, cs] += jnp.sum(gh.reshape(-1, 8, width), axis=0)
            gh_ref[rows, cs] = gh.astype(bf16)
    for m in range(clips):
        rows = slice(m * frames, (m + 1) * frames)
        g = dot(gh_ref[rows], up_ref[...], 1, 1)
        tiles = [slice(c * LANES, (c + 1) * LANES) for c in range(width // LANES)]
        sums = [jnp.zeros((8, LANES), f32)] * len(tiles)
        for r in range(0, frames, TAIL):
            at = slice(m * frames + r, m * frames + r + TAIL)
            gs = [g[r : r + TAIL, cs] * small_ref[GAIN : GAIN + 1, cs] for cs in tiles]
            xs = [xhat_ref[at, cs].astype(f32) for cs in tiles]
            mean = jnp.sum(sum(gs[1:], gs[0]), axis=-1, keepdims=True) / width
            products = [p * q for p, q in zip(gs, xs)]
            proj = jnp.sum(sum(products[1:], products[0]), axis=-1, keepdims=True) / width
            for c in range(len(tiles)):
                gc = (gs[c] - mean - xs[c] * proj) * rstd_ref[at]
                pad_ref[m, c, HALO + r : HALO + r + TAIL] = gc
                sums[c] = sums[c] + jnp.sum(gc.reshape(-1, 8, LANES), axis=0)
        for c, cs in enumerate(tiles):
            tsum_ref[TAPS, :, cs] += sums[c]
    acc_ref[...] += dot(xhat_ref[...], gh_ref[...], 0, 0)
    for m in range(clips):
        keep = tail_mask(frames, lengths[m], LANES)
        for c in range(width // LANES):
            cs = slice(c * LANES, (c + 1) * LANES)
            sums = [jnp.zeros((8, LANES), f32)] * TAPS
            for r in range(0, frames, TAIL):
                x = x_ref[m, r : r + TAIL, cs].astype(f32)
                total = cot_ref[m, r : r + TAIL, cs].astype(f32)
                if r + TAIL == frames:
                    x = jnp.where(keep, x, 0.0)
                for k in range(TAPS):
                    start = HALO + TAPS // 2 - k + r
                    gc = pad_ref[m, c, start : start + TAIL]
                    total = total + small_ref[k : k + 1, cs] * gc
                    sums[k] = sums[k] + jnp.sum((gc * x).reshape(-1, 8, LANES), axis=0)
                if r + TAIL == frames:
                    total = jnp.where(keep, total, 0.0)
                grad_ref[m, r : r + TAIL, cs] = total.astype(bf16)
            for k in range(TAPS):
                tsum_ref[k, :, cs] += sums[k]

    @pl.when(step == pl.num_programs(0) - 1)
    def _():
        total = acc_ref[...]
        hsum = jnp.sum(hsum_ref[...], axis=0, keepdims=True)
        columns = small_ref[...].T
        gain, shift = columns[:, GAIN : GAIN + 1], columns[:, SHIFT : SHIFT + 1]
        rows = [jnp.sum(tsum_ref[k], axis=0, keepdims=True) for k in range(TAPS + 1)]
        up = up_ref[...].astype(f32)
        for value in (up * total, up * hsum):
            part = value[:, :LANES]
            for c in range(1, hidden // LANES):
                part = part + value[:, c * LANES : (c + 1) * LANES]
            rows.append(jnp.sum(part.T, axis=0, keepdims=True))
        rows.append(down_rows_ref[0:2])
        if not packed:
            out_a_ref[...] = (gain * total + shift * hsum).astype(bf16)
            rows += [hsum[:, p * width : (p + 1) * width] for p in range(parts)]
            rows.append(jnp.zeros((SMALL - UP_BIAS - parts, width), f32))
            out_b_ref[...] = jnp.concatenate(rows, axis=0)
            return
        rows.append(jnp.zeros((SMALL - UP_BIAS, width), f32))
        rows = jnp.concatenate(rows, axis=0)
        bias = hsum
        lane = lax.broadcasted_iota(jnp.int32, (SMALL, LANES), 1)
        line = lax.broadcasted_iota(jnp.int32, (SMALL, LANES), 0)
        devices = width // 16
        even = core_ref[0] == 0
        acc_ref[...] = gain * total + shift * hsum
        for chip in range(devices // 2):
            for ref, core in ((out_a_ref, core_ref[0]), (out_b_ref, 1 - core_ref[0])):
                at = pl.multiple_of(chip * 32 + core * 16, 16)
                for c in range(hidden // LANES):
                    value = acc_ref[pl.ds(at, 16), c * LANES : (c + 1) * LANES]
                    ref[chip, c * 16 : (c + 1) * 16] = value.astype(bf16)
        pair = []
        for owner in range(devices):
            at = owner * 16 // LANES * LANES
            mine = pltpu.roll(rows[:, at : at + LANES], (LANES - owner * 16 % LANES) % LANES, 1)
            for r in range(parts):
                first = owner * 16 * parts + r * 16
                at = first // LANES * LANES
                part = pltpu.roll(
                    jnp.broadcast_to(bias[:, at : at + LANES], (SMALL, LANES)), (LANES - first % LANES) % LANES, 1
                )
                mine = jnp.where(line == UP_BIAS + r, part, mine)
            high = mine.astype(bf16).astype(f32)
            low = pltpu.roll(mine - high, LANES // 2, 1)
            pair.append(jnp.where(lane < 16, high, jnp.where((lane >= LANES // 2) & (lane < LANES // 2 + 16), low, 0.0)))
            if owner % 2:
                first, second = pair[-2:]
                out_a_ref[owner // 2, hidden // LANES * 16 :] = jnp.where(even, first, second).astype(bf16)
                out_b_ref[owner // 2, hidden // LANES * 16 :] = jnp.where(even, second, first).astype(bf16)


def first_forward(
    len_ref, x_ref, up_ref, down_ref, small_ref, bias_ref, _, parts_ref, scale_ref,
    out_ref, grad_down_ref,
    pad_ref, xhat_ref, act_ref,
):
    total = jnp.zeros(parts_ref.shape[1:], f32)
    for j in range(parts_ref.shape[0]):
        total = total + parts_ref[j].astype(f32)
    grad_down_ref[...] = total * (scale_ref[SCALE : SCALE + 1] * 0.5)

    step = pl.program_id(0)
    clips, frames, width = x_ref.shape
    parts = up_ref.shape[1] // width

    @pl.when(step == 0)
    def _():
        clear_halo(pad_ref, frames)

    lengths = [len_ref[step * clips + m] for m in range(clips)]
    down_bias = small_ref[DOWN_BIAS : DOWN_BIAS + 1] * small_ref[SCALE : SCALE + 1]

    def front(m):
        fill_padded(x_ref, m, lengths[m], pad_ref)
        xhat_ref[m * frames : (m + 1) * frames] = conv_norm(pad_ref, m, small_ref, frames)

    front(0)
    for m in range(clips):
        if m + 1 < clips:
            front(m + 1)
        rows = slice(m * frames, (m + 1) * frames)
        for p in range(2 * parts):
            cs = slice(p * width // 2, (p + 1) * width // 2)
            u = dot(xhat_ref[rows], up_ref[:, cs]) + bias_ref[0:1, cs]
            act_ref[rows, cs] = (u * (1.0 + lax.erf(u * ROOT))).astype(bf16)
        store_output(out_ref, m, lengths[m], x_ref, dot(act_ref[rows], down_ref[...]) + down_bias)


def kernel_call(body, name, args, specs, outs, scratch, steps, flops, elements):
    def size(a):
        return math.prod(a.shape) * jnp.dtype(a.dtype).itemsize

    return pl.pallas_call(
        body,
        grid=(steps,),
        in_specs=specs,
        out_specs=[spec for _, spec in outs],
        out_shape=[shape for shape, _ in outs],
        scratch_shapes=scratch,
        compiler_params=pltpu.CompilerParams(vmem_limit_bytes=VMEM),
        cost_estimate=pl.CostEstimate(
            flops=flops,
            bytes_accessed=sum(map(size, args)) + sum(size(s) for s, _ in outs),
            transcendentals=elements,
        ),
        name=name,
    )(*args)


def shape(dims, dtype):
    return jax.ShapeDtypeStruct(dims, dtype)


def own_block(
    me_ref, conv_ref, conv_bias_ref, gain_ref, shift_ref, up_ref, up_bias_ref, down_ref, down_bias_ref, scale_ref,
    block_ref,
    row_ref,
):
    own, hidden = up_ref.shape
    rows, width = down_ref.shape
    parts = hidden // width
    me = me_ref[0]
    for p in range(parts):
        block_ref[p * own : (p + 1) * own] = up_ref[:, p * width : (p + 1) * width]
    block_ref[rows : 2 * rows] = down_ref[...]
    vectors = [r[...].astype(f32) for r in (conv_bias_ref, gain_ref, shift_ref, down_bias_ref, scale_ref)]
    small = jnp.concatenate([conv_ref[...].astype(f32)] + vectors + [jnp.zeros((SMALL - UP_BIAS, own), f32)], axis=0)
    small = jnp.concatenate([small, jnp.zeros((SMALL, LANES - own), f32)], axis=1)
    row_ref[...] = jnp.zeros_like(row_ref)
    per = LANES // own
    at = pl.multiple_of(me // per * LANES, LANES)
    row_ref[:, pl.ds(at, LANES)] = pltpu.roll(small, me % per * own, 1)
    bias = jnp.concatenate([up_bias_ref[...].astype(f32), jnp.zeros((1, 2 * LANES - rows), f32)], axis=1)
    bias = pltpu.roll(jnp.broadcast_to(bias, (8, 2 * LANES)), me * rows % LANES, 1)
    first = me * rows // LANES
    tiles = width // LANES
    for t in range(hidden // LANES):
        part = jnp.where(first == t, bias[:1, :LANES], jnp.where(first + 1 == t, bias[:1, LANES:], 0.0))
        row_ref[UP_BIAS + t // tiles : UP_BIAS + t // tiles + 1, t % tiles * LANES : (t % tiles + 1) * LANES] = part

    block_ref[2 * rows :] = row_ref[...].astype(bf16)


def quick(width, hidden, devices):
    return devices == 32 and width == 16 * devices and hidden % width == 0


def flipped(a, bits, devices):
    return lax.ppermute(a, AXES, [(i, i ^ bits) for i in range(devices)])


def gather_weights(weights, devices):
    conv_weight, conv_bias, gain, shift, up, up_bias, down, down_bias, scale = weights
    up_rows, hidden = up.shape
    down_rows, width = down.shape
    parts = hidden // width
    me = lax.axis_index(AXES).astype(jnp.int32)
    if quick(width, hidden, devices):
        row = lambda v: v.reshape(1, -1)
        args = (me.reshape(1), conv_weight, row(conv_bias), row(gain), row(shift), up, row(up_bias), down, row(down_bias), row(scale))
        block = pl.pallas_call(
            own_block,
            in_specs=[smem()] + [pl.BlockSpec(memory_space=pltpu.VMEM)] * 9,
            out_specs=pl.BlockSpec(memory_space=pltpu.VMEM),
            out_shape=shape((2 * down_rows + SMALL, width), bf16),
            scratch_shapes=[pltpu.VMEM((SMALL, width), f32)],
            name="own_block",
        )(*args)
        both = jnp.stack([block, flipped(block, 16, devices)])
        have = {0: both}
        for flip, start in ((8, 0), (4, 0), (2, 0), (2, 4), (8, 2), (4, 8), (8, 6)):
            have[flip ^ start] = flipped(have[start], flip, devices)
        for start in list(have):
            have[start ^ 1] = flipped(have[start], 1, devices)
        order = [start ^ far for start in have for far in (0, 16)]
        return list(have.values()), order, me.reshape(1)
    everyone = lambda a, axis: lax.all_gather(a, AXES, axis=axis, tiled=True)
    up, down, up_bias = everyone(up, 0), everyone(down, 0), everyone(up_bias, 0)
    vectors = jnp.stack([conv_bias, gain, shift, down_bias, scale])
    small = jnp.concatenate([everyone(conv_weight, 1), everyone(vectors, 1), up_bias.reshape(parts, width)], axis=0)
    small = jnp.pad(small, ((0, SMALL - small.shape[0]), (0, 0)))
    count = width // 16
    up = up.reshape(count, 16, parts, width).swapaxes(1, 2).reshape(count, 16 * parts, width)
    down = down.reshape(count, 16 * parts, width)
    small = jnp.pad(small[None], ((0, count - 1), (0, 0), (0, 0)))
    return [jnp.concatenate([up, down, small], axis=1)], list(range(count)), jnp.zeros((1,), jnp.int32)


def finish(parts_ref, grad_up_ref, taps_ref, up_bias_ref, *vector_refs):
    total = jnp.zeros(parts_ref.shape[1:], f32)
    for j in range(parts_ref.shape[0]):
        total = total + parts_ref[j].astype(f32)
    own, hidden = grad_up_ref.shape
    for c in range(hidden // LANES):
        grad_up_ref[:, c * LANES : (c + 1) * LANES] = total[c * own : (c + 1) * own]
    rows = total[hidden // LANES * own :]
    rows = rows + pltpu.roll(rows, LANES // 2, 1)
    taps_ref[...] = rows[:TAPS, :own]
    up_bias_ref[...] = jnp.concatenate(
        [rows[UP_BIAS + p : UP_BIAS + p + 1, :own] for p in range(up_bias_ref.shape[1] // own)], axis=1
    )
    for ref, r in zip(vector_refs, (CONV_BIAS, GAIN, SHIFT, DOWN_BIAS, SCALE)):
        ref[...] = rows[r : r + 1, :own]


def on_device(chips, first_input, second_input, cotangent, lengths, *weights):
    clips, frames, width = second_input.shape
    hidden = weights[6].shape[0] * chips * 2
    tokens = clips * frames
    block = math.gcd(clips, BLOCK)
    steps = clips // block
    rows = block * frames
    core = lax.axis_index("core").astype(jnp.int32)
    matmul = 2 * tokens * width * hidden

    blocks, owners, base = gather_weights(weights, chips * 2)

    clip_spec = pl.BlockSpec((block, frames, width), lambda i: (i, 0, 0))
    half = math.gcd(clips, BLOCK // 2)
    half_clip = pl.BlockSpec((half, frames, width), lambda i: (i, 0, 0))
    last = clips // half - 1
    later_clip = pl.BlockSpec((half, frames, width), lambda i: (jnp.minimum(i + 1, last), 0, 0))
    half_pad = pltpu.VMEM((half, width // LANES, frames + 2 * HALO, LANES), f32)
    half_row = lambda n: pl.BlockSpec((half * frames, n), lambda i: (i, 0))
    clip_out = (shape(second_input.shape, bf16), clip_spec)
    pad = pltpu.VMEM((block, width // LANES, frames + 2 * HALO, LANES), f32)

    second_output, xhat, slope, rstd, up, down, small, bias, gdown, down_grad_rows = kernel_call(
        functools.partial(second_forward, owners),
        "second_forward",
        (lengths, base, second_input, second_input, cotangent, *blocks),
        [smem(), smem(), half_clip, later_clip, half_clip] + [whole(b.shape) for b in blocks],
        [
            (shape(second_input.shape, bf16), half_clip),
            (shape((tokens, width), bf16), half_row(width)),
            (shape((tokens, hidden), bf16), half_row(hidden)),
            (shape((tokens, LANES), f32), half_row(LANES)),
            (shape((width, hidden), bf16), whole((width, hidden))),
            (shape((hidden, width), bf16), whole((hidden, width))),
            (shape((SMALL, width), f32), whole((SMALL, width))),
            (shape((8, hidden), f32), whole((8, hidden))),
            (shape((hidden, width), bf16), whole((hidden, width))),
            (shape((8, width), f32), whole((8, width))),
        ],
        [
            half_pad,
            pltpu.VMEM((half * frames, hidden), bf16),
            pltpu.VMEM((half * frames, width), bf16),
            pltpu.VMEM((width, hidden), f32),
            pltpu.VMEM((8, width), f32),
            pltpu.VMEM((half * frames, width), bf16),
            pltpu.VMEM((half * frames, width), bf16),
            pltpu.VMEM((half * frames, LANES), f32),
        ],
        clips // half,
        3 * matmul,
        2 * tokens * hidden,
    )

    devices = chips * 2
    fast = quick(width, hidden, devices)
    if fast:
        gdown_parts = lax.all_to_all(gdown.reshape(devices, hidden // devices, width), AXES, 0, 0, tiled=True)
        payload = shape((chips, hidden // LANES * 16 + SMALL, LANES), bf16)
        outs = [(payload, whole(payload.shape))] * 2
    else:
        outs = [
            (shape((width, hidden), bf16), whole((width, hidden))),
            (shape((SMALL, width), f32), whole((SMALL, width))),
        ]

    input_grad, out_a, out_b = kernel_call(
        functools.partial(second_backward, fast),
        "second_backward",
        (lengths, core.reshape(1), cotangent, second_input, xhat, slope, rstd, up, down, small, down_grad_rows, gdown),
        [
            smem(), smem(), half_clip, half_clip, half_row(width), half_row(hidden), half_row(LANES),
            whole(up.shape), whole(down.shape), whole(small.shape), whole(down_grad_rows.shape),
            pl.BlockSpec(memory_space=pl.ANY),
        ],
        [
            (shape(second_input.shape, bf16), half_clip),
            *outs,
        ],
        [
            half_pad,
            pltpu.VMEM((half * frames, hidden), bf16),
            pltpu.VMEM((half * frames, width), bf16),
            pltpu.VMEM((width, hidden), f32),
            pltpu.VMEM((8, hidden), f32),
            pltpu.VMEM((TAPS + 1, 8, width), f32),
        ],
        clips // half,
        3 * matmul,
        0,
    )

    if fast:
        got = flipped(out_b, 1, devices)
        got, gdown_parts = lax.optimization_barrier((got, gdown_parts))
        flat = (-1, LANES)
        gup_pair = (out_a.reshape(flat).astype(f32) + got.reshape(flat).astype(f32)).astype(bf16).reshape(out_a.shape)
        gup_parts = lax.all_to_all(gup_pair, CHIPS, 0, 0, tiled=True)
    else:
        gup_pair, gdown_parts = out_a, gdown[None]

    down_shape = gdown_parts.shape
    columns = width // steps if width % (steps * LANES) == 0 else width
    part = lambda i: i if columns < width else 0
    first_output, grad_down = kernel_call(
        first_forward,
        "first_forward",
        (lengths, first_input, up, down, small, bias, gup_pair, gdown_parts, small),
        [
            smem(), clip_spec, whole(up.shape), whole(down.shape), whole(small.shape), whole(bias.shape),
            pl.BlockSpec(memory_space=pl.ANY),
            pl.BlockSpec(down_shape[:2] + (columns,), lambda i: (0, 0, part(i))),
            pl.BlockSpec((SMALL, columns), lambda i: (0, part(i))),
        ],
        [
            clip_out,
            (shape(down_shape[1:], f32), pl.BlockSpec((down_shape[1], columns), lambda i: (0, part(i)))),
        ],
        [pad, pltpu.VMEM((rows, width), bf16), pltpu.VMEM((rows, hidden), bf16)],
        steps,
        2 * matmul,
        tokens * hidden,
    )

    own = width // devices
    if fast:
        vector = shape((1, own), f32)
        grad_up, grad_taps, grad_up_bias, *vectors = pl.pallas_call(
            finish,
            out_shape=[shape((own, hidden), f32), shape((TAPS, own), f32), shape((1, hidden // devices), f32)] + [vector] * 5,
            name="finish",
        )(gup_parts)
        grad_up_bias = grad_up_bias.reshape(-1)
        vectors = [v.reshape(-1) for v in vectors]
    else:
        scatter = lambda a: lax.psum_scatter(a.astype(f32), AXES, scatter_dimension=0, tiled=True)
        me = lax.axis_index(AXES)
        grad_down = scatter(grad_down)
        grad_up = scatter(out_a)
        sums = lax.psum(out_b, AXES)
        vectors = [lax.dynamic_slice(sums[r], (me * own,), (own,)) for r in (CONV_BIAS, GAIN, SHIFT, DOWN_BIAS, SCALE)]
        grad_taps = lax.dynamic_slice(sums, (0, me * own), (TAPS, own))
        grad_up_bias = lax.dynamic_slice(
            sums[UP_BIAS : UP_BIAS + hidden // width].reshape(-1), (me * (hidden // devices),), (hidden // devices,)
        )
    conv_bias, gain, shift, down_bias, scale = vectors
    return (
        first_output,
        second_output,
        input_grad,
        grad_taps,
        conv_bias,
        gain,
        shift,
        grad_up,
        grad_up_bias,
        grad_down,
        down_bias,
        scale,
    )


def solution(mesh):
    wide, narrow = mesh.devices.shape
    grid = Mesh(mesh.devices.reshape(wide, narrow // 2, 2), AXES)
    chips = wide * narrow // 2
    rows = P(AXES)
    columns = P(None, AXES)

    def run(*args):
        return on_device(chips, *args)

    return jax.shard_map(
        run,
        mesh=grid,
        in_specs=(rows, rows, rows, rows, columns, rows, rows, rows, rows, rows, rows, rows, rows),
        out_specs=(rows, rows, rows, columns, rows, rows, rows, rows, rows, rows, rows, rows),
        check_vma=False,
    )
```
